32 devices in a mesh: dp: 8 (over z, x), narrow: 4 (over y, core).
Axes of the slice: x: 2, y: 2, z: 4, core: 2. Of those that a mesh axis runs over, the one named last changes fastest.
Arguments:
- inputs: bfloat16 [32, 512, 768], P(('dp', 'narrow')), may hold values from -6 to 6
- segments: int32 [32, 512], P(('dp', 'narrow')), may hold values from 0 to 3, never falling along the last dimension, each value on 1 to 256 neighbouring positions
- out_grad: bfloat16 [32, 512, 768], P(('dp', 'narrow')), may hold values from -6 to 6
- logit_grad: bfloat16 [32, 12, 512, 512], P(('dp', 'narrow')), may hold values from -0.59765625 to 0.59765625
- w_qkv: float32 [2, 768, 2304], P(None, 'dp', 'narrow'), may hold values from -0.21875 to 0.21875
- w_out: float32 [2, 768, 768], P(None, 'dp', 'narrow'), may hold values from -0.875 to 0.875
- w_up: float32 [2, 768, 3072], P(None, 'dp', 'narrow'), may hold values from -0.21875 to 0.21875
- w_down: float32 [2, 3072, 768], P(None, 'dp', 'narrow'), may hold values from -0.109375 to 0.109375
- biases: float32 [2, 4, 768], replicated, may hold values from -3 to 3
- up_bias: float32 [2, 3072], replicated, may hold values from -3 to 3
- gains: float32 [2, 2, 768], replicated, may hold values from 0.5 to 1.5
- shifts: float32 [2, 2, 768], replicated, may hold values from -1.8 to 1.8
Outputs:
- result: bfloat16 [32, 512, 768], P(('dp', 'narrow'))
- logits: bfloat16 [32, 12, 512, 512], P(('dp', 'narrow'))
- grad_inputs: bfloat16 [32, 512, 768], P(('dp', 'narrow'))
- grad_w_qkv: float32 [2, 768, 2304], P(None, 'dp', 'narrow')
- grad_w_out: float32 [2, 768, 768], P(None, 'dp', 'narrow')
- grad_w_up: float32 [2, 768, 3072], P(None, 'dp', 'narrow')
- grad_w_down: float32 [2, 3072, 768], P(None, 'dp', 'narrow')
- grad_biases: float32 [2, 4, 768], replicated
- grad_up_bias: float32 [2, 3072], replicated
- grad_gains: float32 [2, 2, 768], replicated
- grad_shifts: float32 [2, 2, 768], replicated
The draws below stay inside these ranges and needn't reach their ends.
Inputs may be any that keep to these rules, and one draw needn't show every extreme that they name: `segments`: within a row the numbers never fall, and one number spans 1 to 256 consecutive slots.
All inputs are finite; a program needn't handle non-finite values.
Results may differ from the reference program's by a relative error of at most 0.02.
Values may be sent and summed in bfloat16 or wider, within the bound.
A program may use at most 256 MiB of HBM per device.

```python
import math
import jax
import jax.numpy as jnp
import numpy as np
from jax import lax

D = 768
FF = 3072
HEADS = 12
HEAD_DIM = 64
S = 512
SEGMENTS = 4
LAYERS = 2
ROWS = 32


def shard_levels(stream_key, extent, pieces, least, top_value):
    loudness, own = 1.0, jax.random.fold_in(stream_key, 6)
    for axis_at, blocks in pieces:
        draws = jnp.exp(jax.random.uniform(jax.random.fold_in(own, axis_at), (blocks,), jnp.float32, least / len(pieces), top_value / len(pieces)))
        loudness = loudness * jnp.repeat(draws, extent[axis_at] // blocks).reshape([-1 if axis == axis_at else 1 for axis in range(len(extent))])
    return loudness


def length_profile(number_of, total, limit, slope):
    weights = [(1 << 20) // math.isqrt(standing ** slope) + 1 for standing in range(2, number_of + 1)]
    surplus, given = total - limit - (number_of - 1), [1] * (number_of - 1)
    while surplus > 0:
        free = [i for i in range(number_of - 1) if given[i] < limit]
        mass, budget = sum([weights[i] for i in free]), surplus
        for i in free:
            extra = min(limit - given[i], max(1, budget * weights[i] // mass), surplus)
            given[i] = given[i] + extra
            surplus = surplus - extra
    return np.array([limit] + given)


def ragged(own_key, amount, total, limit, skew):
    if amount == 2:
        one = jax.random.randint(own_key, (), max(1, total - limit), min(limit, total - 1) + 1)
        return jnp.stack([one, total - one])
    sizes = jnp.asarray(length_profile(amount, total, limit, skew), jnp.int32)
    twos = (amount - 1) // 2
    source_of, taker = sizes[1:1 + 2 * twos:2], sizes[2:2 + 2 * twos:2]
    slack = jnp.minimum(source_of - 1, limit - taker)
    shifted = jax.random.randint(jax.random.fold_in(own_key, 1), (twos,), 0, 1 << 20) % (slack + 1)
    sizes = sizes.at[1:1 + 2 * twos:2].set(source_of - shifted).at[2:2 + 2 * twos:2].set(taker + shifted)
    return sizes[jax.random.permutation(jax.random.fold_in(own_key, 2), amount)]


def bell_draw(rng, shape, scale, reach, shards=(), kind=jnp.bfloat16):
    entries = jax.random.normal(rng, shape, jnp.float32) * scale
    if len(shards) > 0:
        entries = shard_levels(rng, shape, shards, -0.22, 0.18) * entries
    return jnp.clip(entries, min=-reach, max=reach).astype(kind)


def setup_inputs(seed: int = 0) -> dict:
    keys = jax.random.split(jax.random.key(seed), 13)
    return {
        "inputs": bell_draw(keys[0], (ROWS, S, D), 1.0, 6.0, ((0, 32),)),
        "segments": jax.vmap(lambda own: jnp.searchsorted(jnp.cumsum(ragged(own, SEGMENTS, S, S // 2, 2)), jnp.arange(S), side="right"))(jax.random.split(keys[1], ROWS)).reshape((ROWS, S)).astype(jnp.int32),
        "out_grad": bell_draw(keys[2], (ROWS, S, D), 1.0, 6.0, ((0, 32),)),
        "logit_grad": bell_draw(keys[3], (ROWS, HEADS, S, S), 0.1, 0.59765625, ((0, 32),)),
        "w_qkv": bell_draw(keys[4], (LAYERS, D, 3 * D), D ** -0.5, 0.21875, ((1, 8), (2, 4)), jnp.float32),
        "w_out": bell_draw(keys[5], (LAYERS, D, D), (D // 16) ** -0.5, 0.875, ((1, 8), (2, 4)), jnp.float32),
        "w_up": bell_draw(keys[6], (LAYERS, D, FF), D ** -0.5, 0.21875, ((1, 8), (2, 4)), jnp.float32),
        "w_down": bell_draw(keys[7], (LAYERS, FF, D), FF ** -0.5, 0.109375, ((1, 8), (2, 4)), jnp.float32),
        "biases": bell_draw(keys[8], (LAYERS, 4, D), 0.5, 3.0, (), jnp.float32),
        "up_bias": bell_draw(keys[9], (LAYERS, FF), 0.5, 3.0, (), jnp.float32),
        "gains": jnp.clip(1.0 + 0.1 * jax.random.normal(keys[10], (LAYERS, 2, D), jnp.float32), 0.5, 1.5),
        "shifts": bell_draw(keys[11], (LAYERS, 2, D), 0.3, 1.8, (), jnp.float32),
    }


@jax.custom_vjp
def low(v):
    return lax.optimization_barrier(v.astype(jnp.bfloat16)).astype(jnp.float32)

@jax.custom_vjp
def low_back(v):
    return v

def low_keep(v):
    return (low(v), None)

def low_pass(kept, grad):
    return (grad,)

def back_keep(v):
    return (v, None)

def back_low(kept, grad):
    return (low(grad),)
low.defvjp(low_keep, low_pass)
low_back.defvjp(back_keep, back_low)
masked_value = -1e+30
epsilon = 1e-06

def matmul(former, latter):
    return jnp.dot(former, latter, precision=lax.Precision.HIGHEST)

def normalize(values, scaling, offset):
    average = lax.optimization_barrier(jnp.mean(values, axis=-1, keepdims=True))
    centred = values - average
    spread = lax.optimization_barrier(jnp.mean(centred * centred, axis=-1, keepdims=True))
    return centred * lax.rsqrt(spread + epsilon) * scaling + offset

def layer_ahead(stream, carried, same_segment, qkv_layer, out_layer, up_layer, down_layer, bias_rows, up_vector, gain_rows, shift_rows):
    row_count, length, feature_count = stream.shape
    head_count = feature_count // HEAD_DIM
    score_scale = HEAD_DIM ** (-0.5)
    split_shape = (row_count, length, head_count, HEAD_DIM)
    flattened = stream.reshape(row_count * length, feature_count)
    projected = matmul(low(flattened), low(qkv_layer))
    queries = low_back(low(projected[:, :feature_count] + bias_rows[0]))
    key_vectors = low_back(low(projected[:, feature_count:2 * feature_count]))
    values = low_back(low(projected[:, 2 * feature_count:] + bias_rows[1]))
    scores = low_back(jnp.einsum('bqhd,bkhd->bhqk', queries.reshape(split_shape), key_vectors.reshape(split_shape), precision=lax.Precision.HIGHEST) * score_scale)
    carried_next = scores + carried
    attention = low(jax.nn.softmax(jnp.where(same_segment[:, None], carried_next, masked_value), axis=-1))
    context = jnp.einsum('bhqk,bkhd->bqhd', attention, values.reshape(split_shape), precision=lax.Precision.HIGHEST)
    context = low_back(low(context.reshape(row_count * length, feature_count)))
    attended = low_back(matmul(context, low(out_layer)) + bias_rows[2])
    normed = normalize(flattened + attended, gain_rows[0], shift_rows[0])
    preact = low_back(matmul(low(normed), low(up_layer)) + up_vector)
    active = low(jax.nn.gelu(preact, approximate=False))
    feed_out = low_back(matmul(active, low(down_layer)) + bias_rows[3])
    result = normalize(normed + feed_out, gain_rows[1], shift_rows[1])
    return (result.reshape(row_count, length, feature_count), carried_next)

def forward(stream, same_segment, w_qkv, w_out, w_up, w_down, biases, up_bias, gains, shifts):
    row_count, length, feature_count = stream.shape
    carried = jnp.zeros((row_count, feature_count // HEAD_DIM, length, length), jnp.float32)
    for layer_index in range(LAYERS):
        stream, carried = layer_ahead(stream, carried, same_segment, w_qkv[layer_index], w_out[layer_index], w_up[layer_index], w_down[layer_index], biases[layer_index], up_bias[layer_index], gains[layer_index], shifts[layer_index])
    return (stream, carried)

def reference(inputs, segments, out_grad, logit_grad, w_qkv, w_out, w_up, w_down, biases, up_bias, gains, shifts):
    group_rows = math.gcd(ROWS, max(1, 4096 // S))
    group_count = ROWS // group_rows
    weights = (w_qkv, w_out, w_up, w_down, biases, up_bias, gains, shifts)

    def one_group(running, step_index):
        first_row = (step_index * group_rows).astype(jnp.int32)
        block_in = lax.dynamic_slice_in_dim(inputs, first_row, group_rows, 0).astype(jnp.float32)
        block_segments = lax.dynamic_slice_in_dim(segments, first_row, group_rows, 0)
        same_segment = block_segments[:, :, None] == block_segments[:, None, :]
        block_out_grad = lax.dynamic_slice_in_dim(out_grad, first_row, group_rows, 0).astype(jnp.float32)
        block_logit_grad = lax.dynamic_slice_in_dim(logit_grad, first_row, group_rows, 0).astype(jnp.float32)

        def wrapped(stream, qkv_in, out_in, up_in, down_in, biases_in, up_bias_in, gains_in, shifts_in):
            return forward(stream, same_segment, qkv_in, out_in, up_in, down_in, biases_in, up_bias_in, gains_in, shifts_in)
        (block_result, block_logits), pullback = jax.vjp(wrapped, block_in, w_qkv, w_out, w_up, w_down, biases, up_bias, gains, shifts)
        gradients = pullback((block_out_grad, block_logit_grad))
        running = tuple((summed + addend for summed, addend in zip(running, gradients[1:])))
        return (running, (block_result.astype(jnp.bfloat16), block_logits.astype(jnp.bfloat16), gradients[0].astype(jnp.bfloat16)))
    initial = tuple((jnp.zeros_like(member) for member in weights))
    running, (results, logit_blocks, input_grads) = lax.scan(one_group, initial, jnp.arange(group_count, dtype=jnp.int32))
    result = results.reshape((ROWS,) + results.shape[2:])
    logits = logit_blocks.reshape((ROWS,) + logit_blocks.shape[2:])
    grad_inputs = input_grads.reshape((ROWS,) + input_grads.shape[2:])
    return (result, logits, grad_inputs, running[0], running[1], running[2], running[3], running[4], running[5], running[6], running[7])
```

```python
import functools

import jax
import jax.numpy as jnp
from jax import lax
import jax.experimental.pallas as pl
import jax.experimental.pallas.tpu as pltpu
from jax.sharding import PartitionSpec as P

BF, F32 = jnp.bfloat16, jnp.float32
MESH = pl.DeviceIdType.MESH
HEAD_DIM = 64
LAYERS = 2
EPS = 1e-6
MASKED = -1e30

LINES = 4
BLOCK = 96
HALF = BLOCK // 2
WIDE = 768
PARTS = 3
PIECE = HALF // PARTS
ROUNDS = 6 * PARTS
AHEAD = 4
SETS = 6


def nn(left, right):
    return lax.dot_general(left, right, (((1,), (0,)), ((), ())), preferred_element_type=F32)


def nt(left, right):
    return lax.dot_general(left, right, (((1,), (1,)), ((), ())), preferred_element_type=F32)


def tn(left, right):
    return lax.dot_general(left, right, (((0,), (0,)), ((), ())), preferred_element_type=F32)


def low_lanes(shape):
    return lax.broadcasted_iota(jnp.int32, shape, len(shape) - 1) % 128 < HEAD_DIM


def turn(tile):
    return pltpu.roll(tile, HEAD_DIM, 1)


class Place:
    def __init__(self, runs):
        d, n = lax.axis_index("dp"), lax.axis_index("narrow")
        self.runs, self.run = runs, d % runs
        self.a, self.b, self.y, self.c = d // runs // 2, d // runs % 2, n // 2, n % 2

    def at(self, a=None, b=None, y=None, c=None):
        a = self.a if a is None else a
        b = self.b if b is None else b
        y = self.y if y is None else y
        c = self.c if c is None else c
        return ((a * 2 + b) * self.runs + self.run, y * 2 + c)

    def peers(self):
        lines = [self.at(a=(self.a + o) % LINES) for o in range(1, LINES)]
        return lines + [self.at(b=1 - self.b), self.at(y=1 - self.y), self.at(c=1 - self.c)]

    def greet(self):
        barrier = pltpu.get_barrier_semaphore()
        peers = self.peers()
        for peer in peers:
            pl.semaphore_signal(barrier, inc=1, device_id=peer, device_id_type=MESH)
        pl.semaphore_wait(barrier, len(peers))


def push(src, dst, send, recv, to):
    pltpu.make_async_remote_copy(
        src_ref=src, dst_ref=dst, send_sem=send, recv_sem=recv, device_id=to, device_id_type=MESH
    ).start()


def wait_for(view, sem):
    pltpu.make_async_copy(view, view, sem).wait()


class Gather:
    def __init__(self, place, whole, send, recv):
        self.p, self.whole, self.send, self.recv = place, whole, send, recv

    def rows(self, t, half):
        return pl.ds(pl.multiple_of(half * HALF + (t % PARTS) * PIECE, 16), PIECE)

    def line(self, t, half, b, y, c):
        return self.whole.at[t // PARTS, :, b, y, c, self.rows(t, half), :]

    def stage1(self, t):
        p = self.p
        for half in range(2):
            mine = self.whole.at[t // PARTS, p.a, p.b, p.y, p.c, self.rows(t, half), :]
            for o in range(1, LINES):
                push(mine, mine, self.send.at[t, half, 0], self.recv.at[t, half, 0], p.at(a=(p.a + o) % LINES))

    def first(self, half):
        p = self.p
        return (1 - p.b, p.y) if half == 0 else (p.b, 1 - p.y)

    def second(self, half):
        p = self.p
        return (p.b, 1 - p.y) if half == 0 else (1 - p.b, p.y)

    def stage2(self, t):
        p = self.p
        for half in range(2):
            some = self.whole.at[t // PARTS, pl.ds(0, LINES - 1), 0, 0, 0, self.rows(t, half), :]
            wait_for(some, self.recv.at[t, half, 0])
            line = self.line(t, half, p.b, p.y, p.c)
            b1, y1 = self.first(half)
            b2, y2 = self.second(half)
            push(line, line, self.send.at[t, half, 1], self.recv.at[t, half, 1], p.at(b=b1, y=y1))
            push(line, line, self.send.at[t, half, 2], self.recv.at[t, half, 2], p.at(b=b2, y=y2))
            push(line, line, self.send.at[t, half, 3], self.recv.at[t, half, 4], p.at(c=1 - p.c))

    def stage3(self, t):
        p = self.p
        for half in range(2):
            b1, y1 = self.first(half)
            b2, y2 = self.second(half)
            line = self.line(t, half, b1, y1, p.c)
            wait_for(line, self.recv.at[t, half, 1])
            push(line, line, self.send.at[t, half, 2], self.recv.at[t, half, 3], p.at(b=b2, y=y2))
            push(line, line, self.send.at[t, half, 3], self.recv.at[t, half, 5], p.at(c=1 - p.c))

    def stage4(self, t):
        p = self.p
        for half in range(2):
            b2, y2 = self.second(half)
            far = self.line(t, half, b2, y2, p.c)
            wait_for(far, self.recv.at[t, half, 2])
            push(far, far, self.send.at[t, half, 3], self.recv.at[t, half, 6], p.at(c=1 - p.c))
            far = self.line(t, half, 1 - p.b, 1 - p.y, p.c)
            wait_for(far, self.recv.at[t, half, 3])
            push(far, far, self.send.at[t, half, 3], self.recv.at[t, half, 6], p.at(c=1 - p.c))

    def stage5(self, t):
        for half in range(2):
            line = self.line(t, half, 0, 0, 0)
            wait_for(line, self.recv.at[t, half, 4])
            wait_for(line, self.recv.at[t, half, 5])
            two = self.whole.at[t // PARTS, :, :, 0, 0, self.rows(t, half), :]
            wait_for(two, self.recv.at[t, half, 6])
            some = self.whole.at[t // PARTS, pl.ds(0, LINES - 1), 0, 0, 0, self.rows(t, half), :]
            wait_for(some, self.send.at[t, half, 0])
            wait_for(line, self.send.at[t, half, 1])
            wait_for(two, self.send.at[t, half, 2])
            four = self.whole.at[t // PARTS, :, :, :, 0, self.rows(t, half), :]
            wait_for(four, self.send.at[t, half, 3])

    def round(self, t):
        @pl.when(t < ROUNDS)
        def _():
            self.stage2(t)

        @pl.when(t + AHEAD < ROUNDS)
        def _():
            self.stage1(t + AHEAD)

        @pl.when((t >= 1) & (t - 1 < ROUNDS))
        def _():
            self.stage3(t - 1)

        @pl.when((t >= 2) & (t - 2 < ROUNDS))
        def _():
            self.stage4(t - 2)

        @pl.when((t >= 3) & (t - 3 < ROUNDS))
        def _():
            self.stage5(t - 3)


class Reduce:
    def __init__(self, place, grads, owned, got1, got2a, got2b, got3, got4, send, recv, free):
        self.p, self.grads, self.owned = place, grads, owned
        self.got1, self.got2, self.got3, self.got4 = got1, (got2a, got2b), got3, got4
        self.send, self.recv, self.free = send, recv, free

    def rows(self, t, half):
        return pl.ds(pl.multiple_of(half * HALF + (t % PARTS) * PIECE, 16), PIECE)

    def mat(self, t):
        return 2 - (t // PARTS) % 3

    def stage1(self, t):
        p, s = self.p, t % SETS

        @pl.when(t >= SETS)
        def _():
            pl.semaphore_wait(self.free.at[s], LINES + 2)

        for half in range(2):
            for y in range(2):
                push(
                    self.grads.at[self.mat(t), :, :, y, 1 - p.c, self.rows(t, half), :],
                    self.got1.at[s, half, y],
                    self.send.at[s, half, 0],
                    self.recv.at[s, half, 0],
                    p.at(c=1 - p.c),
                )

    def stage2(self, t):
        p, s = self.p, t % SETS
        for half in range(2):
            wait_for(self.got1.at[s, half], self.recv.at[s, half, 0])
            rows = self.rows(t, half)
            for y in range(2):
                mine = self.grads[self.mat(t), :, :, y, p.c, rows, :].astype(F32)
                self.got1[s, half, y] = (self.got1[s, half, y].astype(F32) + mine).astype(BF)
            if half == 0:
                push(
                    self.got1.at[s, half, 1 - p.y],
                    self.got2[0].at[s],
                    self.send.at[s, half, 1],
                    self.recv.at[s, half, 1],
                    p.at(y=1 - p.y),
                )
            else:
                push(
                    self.got1.at[s, half, :, :, 1 - p.b],
                    self.got2[1].at[s],
                    self.send.at[s, half, 1],
                    self.recv.at[s, half, 1],
                    p.at(b=1 - p.b),
                )
        for half in range(2):
            wait_for(self.got1.at[s, half], self.send.at[s, half, 0])

    def stage3(self, t):
        p, s = self.p, t % SETS
        for half in range(2):
            got = self.got2[half]
            wait_for(got.at[s], self.recv.at[s, half, 1])
            if half == 0:
                mine = self.got1[s, half, p.y].astype(F32)
                got[s] = (got[s].astype(F32) + mine).astype(BF)
                src, to = got.at[s, :, 1 - p.b], p.at(b=1 - p.b)
            else:
                mine = self.got1[s, half, :, :, p.b].astype(F32)
                got[s] = (got[s].astype(F32) + mine).astype(BF)
                src, to = got.at[s, 1 - p.y], p.at(y=1 - p.y)
            push(src, self.got3.at[s, half], self.send.at[s, half, 2], self.recv.at[s, half, 2], to)

    def stage4(self, t):
        p, s = self.p, t % SETS
        for half in range(2):
            wait_for(self.got3.at[s, half], self.recv.at[s, half, 2])
            mine = self.got2[0][s, :, p.b] if half == 0 else self.got2[1][s, p.y]
            self.got3[s, half] = (self.got3[s, half].astype(F32) + mine.astype(F32)).astype(BF)
            for o in range(1, LINES):
                a = (p.a + o) % LINES
                push(
                    self.got3.at[s, half, a],
                    self.got4.at[s, half, o - 1],
                    self.send.at[s, half, 3],
                    self.recv.at[s, half, 3],
                    p.at(a=a),
                )

    def stage5(self, t):
        p, s = self.p, t % SETS
        for half in range(2):
            wait_for(self.got4.at[s, half], self.recv.at[s, half, 3])
            total = self.got3[s, half, p.a].astype(F32)
            for o in range(LINES - 1):
                total = total + self.got4[s, half, o].astype(F32)
            self.owned[5 - t // PARTS, self.rows(t, half), :] = total
            wait_for(self.got2[half].at[s], self.send.at[s, half, 1])
            wait_for(self.got3.at[s, half], self.send.at[s, half, 2])
            wait_for(self.got4.at[s, half], self.send.at[s, half, 3])

        @pl.when(t + SETS < ROUNDS)
        def _():
            for peer in p.peers():
                pl.semaphore_signal(self.free.at[s], inc=1, device_id=peer, device_id_type=MESH)

    def round(self, t):
        @pl.when(t < ROUNDS)
        def _():
            self.stage1(t)

        @pl.when((t >= 1) & (t - 1 < ROUNDS))
        def _():
            self.stage2(t - 1)

        @pl.when((t >= 2) & (t - 2 < ROUNDS))
        def _():
            self.stage3(t - 2)

        @pl.when((t >= 3) & (t - 3 < ROUNDS))
        def _():
            self.stage4(t - 3)

        @pl.when((t >= 4) & (t - 4 < ROUNDS))
        def _():
            self.stage5(t - 4)


class Clock:
    def __init__(self, transfer):
        self.transfer, self.done = transfer, 0

    def until(self, count):
        if count > self.done:
            start = self.done

            def step(t, _):
                self.transfer.round(t)
                return 0

            lax.fori_loop(start, count, step, 0)
            self.done = count


def gelu_and_slope(values):
    size = jnp.abs(values)
    below = 1.0 + (0.3275911 * 0.7071067811865476) * size
    rough = pl.reciprocal(below, approx=True)
    t = rough * (2.0 - below * rough)
    bell = jnp.exp(-0.5 * values * values)
    poly = t * (
        0.5 * 0.254829592
        + t * (0.5 * -0.284496736 + t * (0.5 * 1.421413741 + t * (0.5 * -1.453152027 + t * (0.5 * 1.061405429))))
    )
    tail = poly * bell
    phi = jnp.where(values < 0, tail, 1.0 - tail)
    return values * phi, phi + values * (bell * 0.3989422804014327)


def standardize(values):
    centred = values - jnp.mean(values, axis=-1, keepdims=True)
    scale = lax.rsqrt(jnp.mean(centred * centred, axis=-1, keepdims=True) + EPS)
    return centred * scale, scale


def load_mat(whole, index, buffer, sem):
    return [
        pltpu.make_async_copy(whole.at[index, :, :, n // 2, n % 2], buffer.at[n], sem.at[n]) for n in range(4)
    ]


def load_down(whole, index, a, buffer, sem):
    out = []
    for n in range(4):
        for h in range(2):
            src = whole.at[index, a, :, n // 2, n % 2, :, pl.ds(h * 384, 384)]
            out.append(pltpu.make_async_copy(src, buffer.at[:, pl.ds(192 * n + BLOCK * h, BLOCK), :], sem))
    return out


def panel(block):
    return block.reshape(WIDE, block.shape[-1])


def forward_kernel(
    runs, weights, x, seg_q, seg_k, bias, up_bias, gain, shift,
    result, logits, soft_out, qkv_out, ctx_out, hid_out, nl_out, act_out, slope_out, n1_out, n2_out, scale_out, *rest
):
    (whole, stream, qkv, ctx, normed, n1, n2, nl, hid, act, slope, penalty, soft, logit, mat_c, mat_u, mat_d,
     load_sem, soft_sem, save_sem, own_sem, send, recv) = rest
    place = Place(runs)
    own = pltpu.make_async_copy(weights, whole.at[:, place.a, place.b, place.y, place.c], own_sem)
    own.start()
    gather = Gather(place, whole, send, recv)
    place.greet()
    own.wait()

    def begin(t, _):
        gather.stage1(t)
        return 0

    lax.fori_loop(0, AHEAD, begin, 0)
    clock = Clock(gather)

    def arrived(index):
        clock.until(PARTS * index + PARTS + 3)

    penalty[...] = jnp.where(seg_q[...] == seg_k[...], 0.0, MASKED)
    stream[...] = x[...].astype(F32)
    saves = {}

    def save(key, src, dst, sem):
        saves[key] = pltpu.make_async_copy(src, dst, sem)
        saves[key].start()

    def saved(key):
        if key in saves:
            saves.pop(key).wait()

    low = low_lanes((1, 128))
    for layer in range(LAYERS):
        base = 3 * layer
        arrived(base)
        loads = load_mat(whole, base, mat_c, load_sem)
        for copy in loads:
            copy.start()
        if layer > 0:
            saved("hid")
        hid[...] = stream[...].astype(BF)
        if layer > 0:
            save("hid", hid, hid_out, save_sem.at[0])
        for copy in loads:
            copy.wait()

        for pair in range(2):
            hidden = hid[...]
            even = nn(hidden, panel(mat_c[2 * pair, :, :, :, 0:640]))
            odd = nn(hidden, panel(mat_c[2 * pair + 1, :, :, :, 0:640]))
            for tile in range(9):
                if tile < 4:
                    value = even[:, tile * 128 : tile * 128 + 128]
                elif tile == 4:
                    value = jnp.where(low, even[:, 512:640], odd[:, 0:128])
                else:
                    value = odd[:, (tile - 4) * 128 : (tile - 4) * 128 + 128]
                group = pair * 9 + tile
                if group < 6:
                    value = (value + bias[layer * 4 : layer * 4 + 1, group * 128 : group * 128 + 128]).astype(BF)
                    value = value * jnp.asarray(HEAD_DIM**-0.5, BF)
                elif group >= 12:
                    value = value + bias[layer * 4 + 1 : layer * 4 + 2, (group - 12) * 128 : (group - 12) * 128 + 128]
                qkv[layer, group] = value.astype(BF)
        save(("qkv", layer), qkv.at[layer], qkv_out.at[layer], save_sem.at[1 + layer])

        if layer > 0:
            saved("ctx")

        def two_heads(pair, _):
            slot = pair % 2

            @pl.when(pair >= 2)
            def _():
                pltpu.make_async_copy(soft.at[slot], soft_out.at[layer, pl.ds(0, 2)], soft_sem.at[0, slot]).wait()
                if layer == LAYERS - 1:
                    pltpu.make_async_copy(logit.at[slot], logits.at[pl.ds(0, 2)], soft_sem.at[1, slot]).wait()

            values = qkv[layer, 12 + pair]
            keys = qkv[layer, 6 + pair]
            if layer > 0:
                keys = jnp.concatenate([qkv[0, 6 + pair], keys], axis=1)
            for part in range(2):
                rows = pl.ds(part * 256, 256)
                parts = []
                for head in range(2):
                    mine = low if head == 0 else ~low
                    query = jnp.where(mine, qkv[layer, pair, rows, :], jnp.zeros((), BF))
                    if layer > 0:
                        before = jnp.where(mine, qkv[0, pair, rows, :], jnp.zeros((), BF))
                        query = jnp.concatenate([before, query], axis=1)
                    scores = nt(query, keys)
                    if layer == LAYERS - 1:
                        logit[slot, head, rows, :] = scores.astype(BF)
                    scores = scores + penalty[rows, :]
                    powers = jnp.exp(scores - jnp.max(scores, axis=-1, keepdims=True))
                    share = (powers * (1.0 / jnp.sum(powers, axis=-1, keepdims=True))).astype(BF)
                    soft[slot, head, rows, :] = share
                    parts.append(nn(share, values))
                ctx[pair, rows, :] = jnp.where(low, parts[0], parts[1]).astype(BF)
            pltpu.make_async_copy(
                soft.at[slot], soft_out.at[layer, pl.ds(pair * 2, 2)], soft_sem.at[0, slot]
            ).start()
            if layer == LAYERS - 1:
                pltpu.make_async_copy(logit.at[slot], logits.at[pl.ds(pair * 2, 2)], soft_sem.at[1, slot]).start()
            return 0

        for third in range(3):
            lax.fori_loop(third * 2, third * 2 + 2, two_heads, 0)
            if third < 2:
                clock.until(min(clock.done + 1, PARTS * 6 + 3))
        for slot in range(2):
            pltpu.make_async_copy(soft.at[slot], soft_out.at[layer, pl.ds(0, 2)], soft_sem.at[0, slot]).wait()
            if layer == LAYERS - 1:
                pltpu.make_async_copy(logit.at[slot], logits.at[pl.ds(0, 2)], soft_sem.at[1, slot]).wait()
        save("ctx", ctx, ctx_out.at[layer], save_sem.at[3])

        context = jnp.concatenate([ctx[pair] for pair in range(6)], axis=1)
        pieces = []
        for pair in range(2):
            even = nn(context, panel(mat_c[2 * pair, :, :, :, 512:768]))
            odd_far = nn(context, panel(mat_c[2 * pair + 1, :, :, :, 640:768]))
            odd_near = nn(context, panel(mat_c[2 * pair + 1, :, :, :, 0:128]))
            pieces += [even[:, 128:256], turn(jnp.where(low, odd_near, even[:, 0:128])), odd_far]
        first_sum = stream[...] + (jnp.concatenate(pieces, axis=1) + bias[layer * 4 + 2 : layer * 4 + 3, :])
        if layer > 0:
            saved("n1")
            saved("nl")
        unit, scale = standardize(first_sum)
        n1[...] = unit
        scale_out[:, 2 * layer : 2 * layer + 1] = scale
        after = unit * gain[2 * layer : 2 * layer + 1, :] + shift[2 * layer : 2 * layer + 1, :]
        normed[...] = after
        nl[...] = after.astype(BF)
        save("n1", n1, n1_out.at[layer], save_sem.at[4])
        save("nl", nl, nl_out.at[layer], save_sem.at[5])

        arrived(base + 1)
        loads = load_mat(whole, base + 1, mat_u, load_sem)
        for copy in loads:
            copy.start()
        if layer > 0:
            saved("act")
            saved("slope")
        for copy in loads:
            copy.wait()

        def widen(n, _):
            pre = nn(nl[...], panel(mat_u[n])) + up_bias[layer * 4 + n]
            value, slant = gelu_and_slope(pre)
            act[n] = value.astype(BF)
            slope[n] = slant.astype(BF)
            return 0

        lax.fori_loop(0, 4, widen, 0)
        save("act", act, act_out.at[layer], save_sem.at[6])
        save("slope", slope, slope_out.at[layer], save_sem.at[7])
        arrived(base + 2)
        loads = [load_down(whole, base + 2, a, mat_d.at[a], load_sem.at[a]) for a in range(LINES)]
        for copies in loads:
            for copy in copies:
                copy.start()
        for a in range(LINES):
            wait_for(mat_d.at[a], load_sem.at[a])
        if layer > 0:
            saved("n2")
        n2[...] = normed[...] + bias[layer * 4 + 3 : layer * 4 + 4, :]

        def narrow_down(a, _):
            for b in range(2):
                n2[...] += nt(act[a, :, b * 384 : b * 384 + 384], mat_d[a, b])
            return 0

        lax.fori_loop(0, LINES, narrow_down, 0)
        unit, scale = standardize(n2[...])
        n2[...] = unit
        scale_out[:, 2 * layer + 1 : 2 * layer + 2] = scale
        after = unit * gain[2 * layer + 1 : 2 * layer + 2, :] + shift[2 * layer + 1 : 2 * layer + 2, :]
        stream[...] = after
        save("n2", n2, n2_out.at[layer], save_sem.at[8])
    result[...] = stream[...].astype(BF)
    for key in list(saves):
        saved(key)
    clock.until(ROUNDS + 3)


def backward_kernel(
    runs, whole, x, hid2, qkv_in, ctx_in, nl_in, act_in, slope_in, n1_in, n2_in, scale_in, soft_in, out_grad, logit_grad,
    gain, *rest
):
    (grad_in, owned, vec, carry, stream, second, acc, go, go_t, nl, nl_t, unit, ctx, gctx, qkv, gqkv, ubuf, dbuf,
     actbuf, slopebuf, soft, dc_in, dc_out, load_sem, misc_sem, soft_sem, grads,
     got1, got2a, got2b, got3, got4, send, recv, free, vec_got, vec_line, vec_send, vec_recv) = rest
    place = Place(runs)
    place.greet()
    clock = Clock(Reduce(place, grads, owned, got1, got2a, got2b, got3, got4, send, recv, free))
    low = low_lanes((1, 128))
    stream[...] = out_grad[...].astype(F32)

    def copies(layer, n, slot):
        y, c = n // 2, n % 2
        return (
            [
                pltpu.make_async_copy(whole.at[3 * layer + 1, :, :, y, c], ubuf.at[slot], load_sem.at[slot, 0]),
                pltpu.make_async_copy(act_in.at[layer, n], actbuf.at[slot], load_sem.at[slot, 1]),
                pltpu.make_async_copy(slope_in.at[layer, n], slopebuf.at[slot], load_sem.at[slot, 2]),
            ],
            load_down(whole, 3 * layer + 2, n, dbuf.at[slot], load_sem.at[slot, 3]),
        )

    def start_all(layer, n, slot):
        some, more = copies(layer, n, slot)
        for copy in some + more:
            copy.start()

    def wait_all(layer, n, slot):
        for copy in copies(layer, n, slot)[0]:
            copy.wait()
        wait_for(dbuf.at[slot], load_sem.at[slot, 3])

    def norm_back(grad, unit, scale, row):
        vec[row[0] : row[0] + 1, :] = jnp.sum(grad * unit, axis=0, keepdims=True)
        vec[row[1] : row[1] + 1, :] = jnp.sum(grad, axis=0, keepdims=True)
        scaled = grad * gain[row[2] : row[2] + 1, :]
        return (
            scaled
            - jnp.mean(scaled, axis=-1, keepdims=True)
            - unit * jnp.mean(scaled * unit, axis=-1, keepdims=True)
        ) * scale

    for layer in reversed(range(LAYERS)):
        base = 12 * layer
        early = [
            pltpu.make_async_copy(n2_in.at[layer], unit, misc_sem.at[0]),
            pltpu.make_async_copy(nl_in.at[layer], nl, misc_sem.at[1]),
            pltpu.make_async_copy(ctx_in.at[layer], ctx, misc_sem.at[2]),
            pltpu.make_async_copy(qkv_in.at[layer], qkv, misc_sem.at[3]),
        ]
        for copy in early:
            copy.start()
        start_all(layer, 0, 0)
        for copy in early[:2]:
            copy.wait()
        if layer == 0:
            clock.until(2 * PARTS + 1)
        second[...] = norm_back(
            stream[...], unit[...], scale_in[:, 2 * layer + 1 : 2 * layer + 2], (base + 9, base + 11, 2 * layer + 1)
        )
        go[...] = second[...].astype(BF)
        go_t[...] = go[...].T
        nl_t[...] = nl[...].T
        late = [
            pltpu.make_async_copy(n1_in.at[layer], unit, misc_sem.at[0]),
            pltpu.make_async_copy(hid2 if layer == 1 else x, nl, misc_sem.at[1]),
        ]
        for copy in late:
            copy.start()
        vec[base + 3 : base + 4, :] = jnp.sum(go[...].astype(F32), axis=0, keepdims=True)
        acc[...] = second[...]

        def chunk(n, _):
            slot = n % 2
            wait_all(layer, n, slot)

            @pl.when(n < 3)
            def _():
                start_all(layer, n + 1, 1 - slot)

            outer = go[...]
            wide = jnp.concatenate([nn(outer, dbuf[slot, 0]), nn(outer, dbuf[slot, 1])], axis=1)
            pre = (wide * slopebuf[slot].astype(F32)).astype(BF)
            vec[pl.ds(base + 4 + n, 1), :] = jnp.sum(pre.astype(F32), axis=0, keepdims=True)
            acc[...] += nt(pre, panel(ubuf[slot]))
            up = nn(nl_t[...], pre).astype(BF)
            grads[1, :, :, n // 2, n % 2] = up.reshape(LINES, 2, BLOCK, WIDE)
            for b in range(2):
                down = nn(go_t[...], actbuf[slot, :, b * 384 : b * 384 + 384]).astype(BF)
                for m in range(4):
                    for h in range(2):
                        grads[2, n, b, m // 2, m % 2, :, h * 384 : h * 384 + 384] = down[
                            192 * m + BLOCK * h : 192 * m + BLOCK * h + BLOCK, :
                        ]
            return 0

        for half in range(2):
            lax.fori_loop(half * 2, half * 2 + 2, chunk, 0)
            if layer == 0 and half == 0:
                clock.until(clock.done + 1)
        if layer == 1:
            clock.until(2)
        else:
            clock.until(min(3 * PARTS + 2, clock.done + 1))

        def side_copy(n):
            return pltpu.make_async_copy(whole.at[3 * layer, :, :, n // 2, n % 2], ubuf.at[n % 2], load_sem.at[n % 2, 0])

        side_copy(0).start()
        side_copy(1).start()
        for copy in late + early[2:]:
            copy.wait()
        second[...] = norm_back(acc[...], unit[...], scale_in[:, 2 * layer : 2 * layer + 1], (base + 8, base + 10, 2 * layer))
        go[...] = second[...].astype(BF)
        vec[base + 2 : base + 3, :] = jnp.sum(go[...].astype(F32), axis=0, keepdims=True)

        def tile_of(index):
            return go[:, index * 128 : index * 128 + 128]

        zero = jnp.zeros((), BF)
        outs = []
        for pair in range(2):
            mixed = turn(tile_of(3 * pair + 1).astype(F32)).astype(BF)
            outs.append((jnp.where(low, zero, mixed), tile_of(3 * pair)))
            outs.append((jnp.where(low, mixed, zero), tile_of(3 * pair + 2)))
        acc[...] = jnp.zeros_like(acc)
        for n in range(4):
            near = slice(512, 640) if n % 2 == 0 else slice(0, 128)
            side_copy(n).wait()
            acc[...] += nt(outs[n][0], panel(ubuf[n % 2, :, :, :, near])) + nt(
                outs[n][1], panel(ubuf[n % 2, :, :, :, 640:768])
            )
            side_copy((n + 2) % 4).start()
        for pair in range(6):
            gctx[pair] = acc[:, pair * 128 : pair * 128 + 128].astype(BF)

        above = logit_grad if layer == LAYERS - 1 else carry

        def fetch(pair, slot):
            return [
                pltpu.make_async_copy(soft_in.at[layer, pl.ds(pair * 2, 2)], soft.at[slot], soft_sem.at[0, slot]),
                pltpu.make_async_copy(above.at[pl.ds(pair * 2, 2)], dc_in.at[slot], soft_sem.at[1, slot]),
            ]

        for copy in fetch(0, 0):
            copy.start()

        def two_heads(pair, _):
            slot = pair % 2
            for copy in fetch(pair, slot):
                copy.wait()

            @pl.when(pair < 5)
            def _():
                for copy in fetch(pair + 1, 1 - slot):
                    copy.start()

            if layer > 0:

                @pl.when(pair >= 2)
                def _():
                    pltpu.make_async_copy(dc_out.at[slot], carry.at[pl.ds(0, 2)], soft_sem.at[2, slot]).wait()

            queries, keys, values, grad = qkv[pair], qkv[6 + pair], qkv[12 + pair], gctx[pair]
            both = grad.astype(F32) * ctx[pair].astype(F32)
            grad_q, grad_k, grad_v = 0.0, 0.0, 0.0
            for head in range(2):
                mine = low if head == 0 else ~low
                own = jnp.where(mine, grad, zero)
                dot = jnp.sum(jnp.where(mine, both, 0.0), axis=-1, keepdims=True)
                share = soft[slot, head]
                inner = nt(own, values)
                scores = (share.astype(F32) * (inner - dot) + dc_in[slot, head].astype(F32)).astype(BF)
                dc_out[slot, head] = scores
                grad_v = grad_v + tn(share, own)
                grad_q = grad_q + nn(scores, jnp.where(mine, keys, zero))
                grad_k = grad_k + tn(scores, jnp.where(mine, queries, zero))
            gqkv[pair] = (grad_q * HEAD_DIM**-0.5).astype(BF)
            gqkv[6 + pair] = grad_k.astype(BF)
            gqkv[12 + pair] = grad_v.astype(BF)
            if layer > 0:
                pltpu.make_async_copy(dc_out.at[slot], carry.at[pl.ds(pair * 2, 2)], soft_sem.at[2, slot]).start()
            return 0

        for third in range(3):
            lax.fori_loop(third * 2, third * 2 + 2, two_heads, 0)
            if third < 2:
                clock.until(min(clock.done + 1, (2 if layer == 1 else 5) * PARTS))
        if layer > 0:
            for slot in range(2):
                pltpu.make_async_copy(dc_out.at[slot], carry.at[pl.ds(0, 2)], soft_sem.at[2, slot]).wait()
        for group in range(6):
            lanes = slice(group * 128, group * 128 + 128)
            vec[base : base + 1, lanes] = jnp.sum(gqkv[group].astype(F32), axis=0, keepdims=True)
            vec[base + 1 : base + 2, lanes] = jnp.sum(gqkv[12 + group].astype(F32), axis=0, keepdims=True)

        nl_t[...] = nl[...].T
        go_t[...] = jnp.concatenate([ctx[pair] for pair in range(6)], axis=1).T
        stream[...] = second[...]
        for n in range(4):
            pair = n // 2
            if n % 2 == 0:
                tiles = [gqkv[9 * pair + k] for k in range(4)] + [jnp.where(low, gqkv[9 * pair + 4], zero)]
            else:
                tiles = [jnp.where(low, zero, gqkv[9 * pair + 4])] + [gqkv[9 * pair + k] for k in range(5, 9)]
            side = jnp.concatenate(tiles, axis=1)
            side_copy(n).wait()
            stream[...] += nt(side, panel(ubuf[n % 2, :, :, :, 0:640]))
            if n < 2:
                side_copy(n + 2).start()
            first = nn(nl_t[...], side)
            near = nn(go_t[...], outs[n][0])
            far = nn(go_t[...], outs[n][1])
            shape = (LINES, 2, BLOCK, 128)
            mixed = 4 if n % 2 == 0 else 0
            for tile in range(5):
                value = first[:, tile * 128 : tile * 128 + 128]
                if tile == mixed:
                    value = value + near
                grads[0, :, :, n // 2, n % 2, :, tile * 128 : tile * 128 + 128] = value.astype(BF).reshape(shape)
            grads[0, :, :, n // 2, n % 2, :, 640:768] = far.astype(BF).reshape(shape)
        if layer == 1:
            clock.until(2 * PARTS + 1)
    grad_in[...] = stream[...].astype(BF)
    clock.until(ROUNDS)
    steps = [place.at(c=1 - place.c), place.at(y=1 - place.y), place.at(b=1 - place.b)]
    for k, to in enumerate(steps):
        push(vec, vec_got.at[k], vec_send.at[k], vec_recv.at[k], to)
        clock.until(ROUNDS + k + 1)
        wait_for(vec, vec_send.at[k])
        wait_for(vec_got.at[k], vec_recv.at[k])
        vec[...] += vec_got[k]
    for o in range(1, LINES):
        push(vec, vec_line.at[place.a], vec_send.at[3], vec_recv.at[3], place.at(a=(place.a + o) % LINES))
    clock.until(ROUNDS + 4)
    wait_for(vec_line.at[pl.ds(0, LINES - 1)], vec_send.at[3])
    wait_for(vec_line.at[pl.ds(0, LINES - 1)], vec_recv.at[3])
    vec_line[place.a] = vec[...]
    vec[...] = (vec_line[0] + vec_line[1]) + (vec_line[2] + vec_line[3])


def forward(runs, weights, x, segments, bias, up_bias, gain, shift):
    length, width = x.shape
    heads = width // HEAD_DIM
    sds = jax.ShapeDtypeStruct
    vmem, hbm = pl.BlockSpec(memory_space=pltpu.VMEM), pl.BlockSpec(memory_space=pltpu.HBM)
    outs = [
        (sds((length, width), BF), vmem),
        (sds((heads, length, length), BF), hbm),
        (sds((LAYERS, heads, length, length), BF), hbm),
        (sds((LAYERS, 18, length, 128), BF), hbm),
        (sds((LAYERS, 6, length, 128), BF), hbm),
        (sds((length, width), BF), hbm),
        (sds((LAYERS, length, width), BF), hbm),
        (sds((LAYERS, 4, length, width), BF), hbm),
        (sds((LAYERS, 4, length, width), BF), hbm),
        (sds((LAYERS, length, width), F32), hbm),
        (sds((LAYERS, length, width), F32), hbm),
        (sds((length, 2 * LAYERS), F32), vmem),
    ]
    outs.append((sds((6, LINES, 2, 2, 2, BLOCK, WIDE), BF), hbm))
    dma = pltpu.SemaphoreType.DMA
    scratch = [
        pltpu.VMEM((length, width), F32),
        pltpu.VMEM((LAYERS, 18, length, 128), BF),
        pltpu.VMEM((6, length, 128), BF),
        pltpu.VMEM((length, width), F32),
        pltpu.VMEM((length, width), F32),
        pltpu.VMEM((length, width), F32),
        pltpu.VMEM((length, width), BF),
        pltpu.VMEM((length, width), BF),
        pltpu.VMEM((4, length, width), BF),
        pltpu.VMEM((4, length, width), BF),
        pltpu.VMEM((length, length), F32),
        pltpu.VMEM((2, 2, length, length), BF),
        pltpu.VMEM((2, 2, length, length), BF),
        pltpu.VMEM((4, LINES, 2, BLOCK, WIDE), BF),
        pltpu.VMEM((4, LINES, 2, BLOCK, WIDE), BF),
        pltpu.VMEM((LINES, 2, WIDE, 384), BF),
        dma((4,)),
        dma((2, 2)),
        dma((9,)),
        dma(()),
        dma((ROUNDS, 2, 4)),
        dma((ROUNDS, 2, 7)),
    ]
    return pl.pallas_call(
        functools.partial(forward_kernel, runs),
        out_shape=[o[0] for o in outs],
        in_specs=[hbm] + [vmem] * 7,
        out_specs=[o[1] for o in outs],
        scratch_shapes=scratch,
        compiler_params=pltpu.CompilerParams(vmem_limit_bytes=60 << 20, collective_id=0, has_side_effects=True),
        name="ahead",
    )(
        weights, x, segments.reshape(length, 1), segments.reshape(1, length), bias.reshape(-1, width),
        up_bias.reshape(LAYERS * 4, 1, width), gain.reshape(-1, width), shift.reshape(-1, width),
    )


def backward(runs, whole, x, kept, out_grad, logit_grad, gain):
    soft, qkv, ctx, hid2, nl, act, slope, n1, n2, scale = kept
    length, width = x.shape
    heads = width // HEAD_DIM
    sds = jax.ShapeDtypeStruct
    vmem, hbm = pl.BlockSpec(memory_space=pltpu.VMEM), pl.BlockSpec(memory_space=pltpu.HBM)
    blocks = (LINES, 2, 2, 2, BLOCK, WIDE)
    outs = [
        (sds((length, width), BF), vmem),
        (sds((6, BLOCK, WIDE), F32), vmem),
        (sds((12 * LAYERS, width), F32), vmem),
        (sds((heads, length, length), BF), hbm),
    ]
    dma = pltpu.SemaphoreType.DMA
    scratch = [
        pltpu.VMEM((length, width), F32),
        pltpu.VMEM((length, width), F32),
        pltpu.VMEM((length, width), F32),
        pltpu.VMEM((length, width), BF),
        pltpu.VMEM((width, length), BF),
        pltpu.VMEM((length, width), BF),
        pltpu.VMEM((width, length), BF),
        pltpu.VMEM((length, width), F32),
        pltpu.VMEM((6, length, 128), BF),
        pltpu.VMEM((6, length, 128), BF),
        pltpu.VMEM((18, length, 128), BF),
        pltpu.VMEM((18, length, 128), BF),
        pltpu.VMEM((2, LINES, 2, BLOCK, WIDE), BF),
        pltpu.VMEM((2, 2, WIDE, 384), BF),
        pltpu.VMEM((2, length, width), BF),
        pltpu.VMEM((2, length, width), BF),
        pltpu.VMEM((2, 2, length, length), BF),
        pltpu.VMEM((2, 2, length, length), BF),
        pltpu.VMEM((2, 2, length, length), BF),
        dma((2, 4)),
        dma((4,)),
        dma((3, 2)),
        pltpu.VMEM((3,) + blocks, BF),
        pltpu.VMEM((SETS, 2, 2, LINES, 2, PIECE, WIDE), BF),
        pltpu.VMEM((SETS, LINES, 2, PIECE, WIDE), BF),
        pltpu.VMEM((SETS, 2, LINES, PIECE, WIDE), BF),
        pltpu.VMEM((SETS, 2, LINES, PIECE, WIDE), BF),
        pltpu.VMEM((SETS, 2, LINES - 1, PIECE, WIDE), BF),
        dma((SETS, 2, 4)),
        dma((SETS, 2, 4)),
        pltpu.SemaphoreType.REGULAR((SETS,)),
        pltpu.VMEM((3, 12 * LAYERS, width), F32),
        pltpu.VMEM((LINES, 12 * LAYERS, width), F32),
        dma((4,)),
        dma((4,)),
    ]
    return pl.pallas_call(
        functools.partial(backward_kernel, runs),
        out_shape=[o[0] for o in outs],
        in_specs=[hbm] * 10 + [vmem, hbm, vmem, hbm, vmem],
        out_specs=[o[1] for o in outs],
        scratch_shapes=scratch,
        compiler_params=pltpu.CompilerParams(vmem_limit_bytes=62 << 20, collective_id=1, has_side_effects=True),
        name="back",
    )(whole, x, hid2, qkv, ctx, nl, act, slope, n1, n2, scale, soft, out_grad, logit_grad, gain.reshape(-1, width))


def join(qkv, out, odd):
    even_form = jnp.concatenate([qkv, out[..., 128:], out[..., :128]], axis=-1)
    odd_form = jnp.concatenate([out[..., :64], qkv, out[..., 64:]], axis=-1)
    return jnp.where(odd, odd_form, even_form)


def part(block, odd):
    qkv = jnp.where(odd, block[..., 64:640], block[..., :576])
    out_even = jnp.concatenate([block[..., 640:], block[..., 576:640]], axis=-1)
    out_odd = jnp.concatenate([block[..., :64], block[..., 640:]], axis=-1)
    return qkv, jnp.where(odd, out_odd, out_even)


def fold(down):
    lead = down.shape[:-2]
    down = jnp.swapaxes(down, -1, -2).reshape(lead + (2, BLOCK, 384))
    return jnp.swapaxes(down, -2, -3).reshape(lead + (BLOCK, WIDE))


def unfold(block):
    lead = block.shape[:-2]
    block = jnp.swapaxes(block.reshape(lead + (BLOCK, 2, 384)), -2, -3)
    return jnp.swapaxes(block.reshape(lead + (192, 384)), -1, -2)


def body(runs, inputs, segments, out_grad, logit_grad, w_qkv, w_out, w_up, w_down, biases, up_bias, gains, shifts):
    mats = [w.astype(BF) for w in (w_qkv, w_out, w_up, w_down)]
    groups = [[g * runs + r for r in range(runs)] for g in range(2 * LINES)]
    if runs > 1:
        mats = [lax.all_gather(w, "dp", axis_index_groups=groups, axis=1, tiled=True) for w in mats]
    odd = lax.axis_index("narrow") % 2 == 1
    weights = jnp.stack([join(mats[0], mats[1], odd), mats[2], fold(mats[3])], axis=1).reshape(6, BLOCK, WIDE)
    result, logits, *kept, whole = forward(runs, weights, inputs[0], segments, biases, up_bias, gains, shifts)
    grad_in, owned, vec, _ = backward(runs, whole, inputs[0], kept, out_grad[0], logit_grad[0], gains)
    owned = owned.reshape(LAYERS, 3, BLOCK, WIDE)
    g_qkv, g_out = part(owned[:, 0], odd)
    grads = [g_qkv, g_out, owned[:, 1], unfold(owned[:, 2])]
    if runs > 1:
        grads = [
            lax.psum_scatter(g, "dp", axis_index_groups=groups, scatter_dimension=1, tiled=True) for g in grads
        ]
        vec = lax.psum(vec, "dp", axis_index_groups=groups)
    vec = vec.reshape(LAYERS, 12, WIDE)
    return (
        result[None],
        logits[None],
        grad_in[None],
        *grads,
        vec[:, :4],
        vec[:, 4:8].reshape(LAYERS, 4 * WIDE),
        vec[:, 8:10],
        vec[:, 10:12],
    )


def solution(mesh):
    rows = P(("dp", "narrow"), None, None)
    heads = P(("dp", "narrow"), None, None, None)
    blocks = P(None, "dp", "narrow")
    runs = mesh.shape["dp"] // (2 * LINES)
    return jax.shard_map(
        functools.partial(body, runs),
        mesh=mesh,
        in_specs=(rows, P(("dp", "narrow"), None), rows, heads) + (blocks,) * 4 + (P(),) * 4,
        out_specs=(rows, heads, rows) + (blocks,) * 4 + (P(),) * 4,
        check_vma=False,
    )
```

```python
import functools

import jax
import jax.numpy as jnp
from jax import lax
import jax.experimental.pallas as pl
import jax.experimental.pallas.tpu as pltpu
from jax.sharding import PartitionSpec as P

BF, F32 = jnp.bfloat16, jnp.float32
MESH = pl.DeviceIdType.MESH
HEAD_DIM = 64
LAYERS = 2
EPS = 1e-6
MASKED = -1e30

LINES = 4
BLOCK = 96
HALF = BLOCK // 2
WIDE = 768
PARTS = 3
PIECE = HALF // PARTS
ROUNDS = 6 * PARTS
AHEAD = 4
GAP = 0
SETS = 6


def nn(left, right):
    return lax.dot_general(left, right, (((1,), (0,)), ((), ())), preferred_element_type=F32)


def nt(left, right):
    return lax.dot_general(left, right, (((1,), (1,)), ((), ())), preferred_element_type=F32)


def tn(left, right):
    return lax.dot_general(left, right, (((0,), (0,)), ((), ())), preferred_element_type=F32)


def low_lanes(shape):
    return lax.broadcasted_iota(jnp.int32, shape, len(shape) - 1) % 128 < HEAD_DIM


def turn(tile):
    return pltpu.roll(tile, HEAD_DIM, 1)


class Place:
    def __init__(self, runs):
        d, n = lax.axis_index("dp"), lax.axis_index("narrow")
        self.runs, self.run = runs, d % runs
        self.a, self.b, self.y, self.c = d // runs // 2, d // runs % 2, n // 2, n % 2

    def at(self, a=None, b=None, y=None, c=None):
        a = self.a if a is None else a
        b = self.b if b is None else b
        y = self.y if y is None else y
        c = self.c if c is None else c
        return ((a * 2 + b) * self.runs + self.run, y * 2 + c)

    def peers(self):
        lines = [self.at(a=(self.a + o) % LINES) for o in range(1, LINES)]
        return lines + [self.at(b=1 - self.b), self.at(y=1 - self.y), self.at(c=1 - self.c)]

    def greet(self):
        for peer in self.peers():
            pl.semaphore_signal(pltpu.get_barrier_semaphore(), inc=1, device_id=peer, device_id_type=MESH)

    def meet(self):
        pl.semaphore_wait(pltpu.get_barrier_semaphore(), len(self.peers()))


def push(src, dst, send, recv, to):
    pltpu.make_async_remote_copy(
        src_ref=src, dst_ref=dst, send_sem=send, recv_sem=recv, device_id=to, device_id_type=MESH
    ).start()


def wait_for(view, sem):
    pltpu.make_async_copy(view, view, sem).wait()


class Gather:
    def __init__(self, place, whole, send, recv):
        self.p, self.whole, self.send, self.recv = place, whole, send, recv

    def rows(self, t, half):
        return pl.ds(pl.multiple_of(half * HALF + (t % PARTS) * PIECE, 16), PIECE)

    def line(self, t, half, b, y, c):
        return self.whole.at[t // PARTS, :, b, y, c, self.rows(t, half), :]

    def stage1(self, t):
        p = self.p
        for half in range(2):
            mine = self.whole.at[t // PARTS, p.a, p.b, p.y, p.c, self.rows(t, half), :]
            for o in range(1, LINES):
                push(mine, mine, self.send.at[t, half, 0], self.recv.at[t, half, 0], p.at(a=(p.a + o) % LINES))

    def first(self, half):
        p = self.p
        return (1 - p.b, p.y) if half == 0 else (p.b, 1 - p.y)

    def second(self, half):
        p = self.p
        return (p.b, 1 - p.y) if half == 0 else (1 - p.b, p.y)

    def stage2(self, t):
        p = self.p
        for half in range(2):
            some = self.whole.at[t // PARTS, pl.ds(0, LINES - 1), 0, 0, 0, self.rows(t, half), :]
            wait_for(some, self.recv.at[t, half, 0])
            line = self.line(t, half, p.b, p.y, p.c)
            b1, y1 = self.first(half)
            b2, y2 = self.second(half)
            push(line, line, self.send.at[t, half, 1], self.recv.at[t, half, 1], p.at(b=b1, y=y1))
            push(line, line, self.send.at[t, half, 2], self.recv.at[t, half, 2], p.at(b=b2, y=y2))
            push(line, line, self.send.at[t, half, 3], self.recv.at[t, half, 4], p.at(c=1 - p.c))

    def stage3(self, t):
        p = self.p
        for half in range(2):
            b1, y1 = self.first(half)
            b2, y2 = self.second(half)
            line = self.line(t, half, b1, y1, p.c)
            wait_for(line, self.recv.at[t, half, 1])
            push(line, line, self.send.at[t, half, 2], self.recv.at[t, half, 3], p.at(b=b2, y=y2))
            push(line, line, self.send.at[t, half, 3], self.recv.at[t, half, 5], p.at(c=1 - p.c))

    def stage4(self, t):
        p = self.p
        for half in range(2):
            b2, y2 = self.second(half)
            far = self.line(t, half, b2, y2, p.c)
            wait_for(far, self.recv.at[t, half, 2])
            push(far, far, self.send.at[t, half, 3], self.recv.at[t, half, 6], p.at(c=1 - p.c))
            far = self.line(t, half, 1 - p.b, 1 - p.y, p.c)
            wait_for(far, self.recv.at[t, half, 3])
            push(far, far, self.send.at[t, half, 3], self.recv.at[t, half, 6], p.at(c=1 - p.c))

    def stage5(self, t):
        for half in range(2):
            line = self.line(t, half, 0, 0, 0)
            wait_for(line, self.recv.at[t, half, 4])
            wait_for(line, self.recv.at[t, half, 5])
            two = self.whole.at[t // PARTS, :, :, 0, 0, self.rows(t, half), :]
            wait_for(two, self.recv.at[t, half, 6])
            some = self.whole.at[t // PARTS, pl.ds(0, LINES - 1), 0, 0, 0, self.rows(t, half), :]
            wait_for(some, self.send.at[t, half, 0])
            wait_for(line, self.send.at[t, half, 1])
            wait_for(two, self.send.at[t, half, 2])
            four = self.whole.at[t // PARTS, :, :, :, 0, self.rows(t, half), :]
            wait_for(four, self.send.at[t, half, 3])

    def round(self, t):
        @pl.when(t < ROUNDS)
        def _():
            self.stage2(t)

        @pl.when(t + AHEAD < ROUNDS)
        def _():
            self.stage1(t + AHEAD)

        @pl.when((t >= 1) & (t - 1 < ROUNDS))
        def _():
            self.stage3(t - 1)

        @pl.when((t >= 2 + PARTS) & (t - 2 < ROUNDS))
        def _():
            self.stage4(t - 2)

        @pl.when((t >= 3 + PARTS) & (t - 3 < ROUNDS))
        def _():
            self.stage5(t - 3)

    def begin(self):
        def loop(start, stop, stage):
            def step(t, _):
                stage(t)
                return 0

            lax.fori_loop(start, stop, step, 0)

        loop(0, PARTS, self.stage1)
        loop(0, PARTS, self.stage2)
        loop(PARTS, PARTS + 1 + AHEAD, self.stage1)
        loop(0, PARTS, self.stage3)
        self.stage2(PARTS)
        loop(0, PARTS, self.stage4)
        loop(0, PARTS, self.stage5)
        return PARTS + 1


class Reduce:
    def __init__(self, place, grads, owned, got1, got2a, got2b, got3, got4, send, recv, free):
        self.p, self.grads, self.owned = place, grads, owned
        self.got1, self.got2, self.got3, self.got4 = got1, (got2a, got2b), got3, got4
        self.send, self.recv, self.free = send, recv, free

    def rows(self, t, half):
        return pl.ds(pl.multiple_of(half * HALF + (t % PARTS) * PIECE, 16), PIECE)

    def mat(self, t):
        return 2 - (t // PARTS) % 3

    def stage1(self, t):
        p, s = self.p, t % SETS

        @pl.when(t >= SETS)
        def _():
            pl.semaphore_wait(self.free.at[s], LINES + 2)

        for half in range(2):
            for y in range(2):
                push(
                    self.grads.at[self.mat(t), :, :, y, 1 - p.c, self.rows(t, half), :],
                    self.got1.at[s, half, y],
                    self.send.at[s, half, 0],
                    self.recv.at[s, half, 0],
                    p.at(c=1 - p.c),
                )

    def stage2(self, t):
        p, s = self.p, t % SETS
        for half in range(2):
            wait_for(self.got1.at[s, half], self.recv.at[s, half, 0])
            rows = self.rows(t, half)
            for y in range(2):
                self.got1[s, half, y] = self.got1[s, half, y] + self.grads[self.mat(t), :, :, y, p.c, rows, :]
            if half == 0:
                push(
                    self.got1.at[s, half, 1 - p.y],
                    self.got2[0].at[s],
                    self.send.at[s, half, 1],
                    self.recv.at[s, half, 1],
                    p.at(y=1 - p.y),
                )
            else:
                push(
                    self.got1.at[s, half, :, :, 1 - p.b],
                    self.got2[1].at[s],
                    self.send.at[s, half, 1],
                    self.recv.at[s, half, 1],
                    p.at(b=1 - p.b),
                )
        for half in range(2):
            wait_for(self.got1.at[s, half], self.send.at[s, half, 0])

    def stage3(self, t):
        p, s = self.p, t % SETS
        for half in range(2):
            got = self.got2[half]
            wait_for(got.at[s], self.recv.at[s, half, 1])
            if half == 0:
                got[s] = got[s] + self.got1[s, half, p.y]
                src, to = got.at[s, :, 1 - p.b], p.at(b=1 - p.b)
            else:
                got[s] = got[s] + self.got1[s, half, :, :, p.b]
                src, to = got.at[s, 1 - p.y], p.at(y=1 - p.y)
            push(src, self.got3.at[s, half], self.send.at[s, half, 2], self.recv.at[s, half, 2], to)

    def stage4(self, t):
        p, s = self.p, t % SETS
        for half in range(2):
            wait_for(self.got3.at[s, half], self.recv.at[s, half, 2])
            mine = self.got2[0][s, :, p.b] if half == 0 else self.got2[1][s, p.y]
            self.got3[s, half] = self.got3[s, half] + mine
            for o in range(1, LINES):
                a = (p.a + o) % LINES
                push(
                    self.got3.at[s, half, a],
                    self.got4.at[s, half, o - 1],
                    self.send.at[s, half, 3],
                    self.recv.at[s, half, 3],
                    p.at(a=a),
                )

    def stage5(self, t):
        p, s = self.p, t % SETS
        for half in range(2):
            wait_for(self.got4.at[s, half], self.recv.at[s, half, 3])
            total = self.got3[s, half, p.a].astype(F32)
            for o in range(LINES - 1):
                total = total + self.got4[s, half, o].astype(F32)
            self.owned[5 - t // PARTS, self.rows(t, half), :] = total
            wait_for(self.got2[half].at[s], self.send.at[s, half, 1])
            wait_for(self.got3.at[s, half], self.send.at[s, half, 2])
            wait_for(self.got4.at[s, half], self.send.at[s, half, 3])

        @pl.when(t + SETS < ROUNDS)
        def _():
            for peer in p.peers():
                pl.semaphore_signal(self.free.at[s], inc=1, device_id=peer, device_id_type=MESH)

    def round(self, v):
        last = ROUNDS - PARTS
        for lag, stage in enumerate((self.stage1, self.stage2, self.stage3, self.stage4, self.stage5)):
            t = v - lag

            @pl.when((t >= 0) & (t < last))
            def _(stage=stage, t=t):
                stage(t)

            @pl.when((t >= last + GAP) & (t < ROUNDS + GAP))
            def _(stage=stage, t=t):
                stage(t - GAP)


class Clock:
    def __init__(self, transfer):
        self.transfer, self.done = transfer, 0

    def until(self, count):
        if count > self.done:

            def step(t, _):
                self.transfer.round(t)
                return 0

            lax.fori_loop(self.done, count, step, 0)
            self.done = count

    def loop(self, count, work, rounds):
        start = self.done

        def step(i, _):
            work(i)
            if rounds > 0:

                @pl.when(((i + 1) * rounds) // count > (i * rounds) // count)
                def _():
                    self.transfer.round(start + (i * rounds) // count)

            return 0

        lax.fori_loop(0, count, step, 0)
        self.done = start + rounds


def gelu_and_slope(values):
    size = jnp.abs(values)
    below = 1.0 + (0.3275911 * 0.7071067811865476) * size
    rough = pl.reciprocal(below, approx=True)
    t = rough * (2.0 - below * rough)
    bell = jnp.exp(-0.5 * values * values)
    poly = t * (
        0.5 * 0.254829592
        + t * (0.5 * -0.284496736 + t * (0.5 * 1.421413741 + t * (0.5 * -1.453152027 + t * (0.5 * 1.061405429))))
    )
    tail = poly * bell
    phi = jnp.where(values < 0, tail, 1.0 - tail)
    return values * phi, phi + values * (bell * 0.3989422804014327)


def standardize(values):
    centred = values - jnp.mean(values, axis=-1, keepdims=True)
    scale = lax.rsqrt(jnp.mean(centred * centred, axis=-1, keepdims=True) + EPS)
    return centred * scale, scale


def load_mat(whole, index, buffer, sem):
    return [
        pltpu.make_async_copy(whole.at[index, :, :, n // 2, n % 2], buffer.at[n], sem.at[n]) for n in range(4)
    ]


def load_down(whole, index, a, buffer, sem):
    out = []
    for n in range(4):
        for h in range(2):
            src = whole.at[index, a, :, n // 2, n % 2, :, pl.ds(h * 384, 384)]
            out.append(pltpu.make_async_copy(src, buffer.at[:, pl.ds(192 * n + BLOCK * h, BLOCK), :], sem))
    return out


def panel(block):
    return block.reshape(WIDE, block.shape[-1])


def forward_kernel(
    runs, w_qkv, w_out, w_up, w_down, x, segments, bias, up_bias, gain, shift,
    result, logits, soft_out, qkv_out, ctx_out, hid_out, nl_out, act_out, slope_out, n1_out, n2_out, scale_out, *rest
):
    (whole, stream, qkv, ctx, normed, n1, n2, nl, hid, act, slope, penalty, soft, logit, mat_c, mat_u, mat_d,
     load_sem, soft_sem, save_sem, own_sem, send, recv, own, pad_qkv, pad_out) = rest
    place = Place(runs)
    place.greet()
    odd = lax.broadcasted_iota(jnp.int32, (1, 128), 1) * 0 + place.c == 1
    low = low_lanes((1, 128))
    for layer in range(LAYERS):
        pad_qkv[:, 0:576] = w_qkv[layer].astype(F32)
        pad_out[:, 0:192] = w_out[layer].astype(F32)
        plain = pad_qkv[...]
        moved = pltpu.roll(plain, HEAD_DIM, 1)
        near, far = pad_out[:, 0:128], pad_out[:, 128:256]
        tiles = [(plain[:, k * 128 : k * 128 + 128], moved[:, k * 128 : k * 128 + 128]) for k in range(5)]
        tiles[4] = (jnp.where(low, tiles[4][0], turn(far)), tiles[4][1])
        tiles[0] = (tiles[0][0], jnp.where(low, near, tiles[0][1]))
        tiles.append((near, jnp.where(low, turn(near), turn(far))))
        for k, (even_form, odd_form) in enumerate(tiles):
            own[3 * layer, :, k * 128 : k * 128 + 128] = jnp.where(odd, odd_form, even_form).astype(BF)
        own[3 * layer + 1] = w_up[layer].astype(BF)
        own[3 * layer + 2, :, 0:384] = w_down[layer, 0:BLOCK, :].astype(BF)
        own[3 * layer + 2, :, 384:768] = w_down[layer, BLOCK : 2 * BLOCK, :].astype(BF)
    own_copy = pltpu.make_async_copy(own, whole.at[:, place.a, place.b, place.y, place.c], own_sem)
    own_copy.start()
    gather = Gather(place, whole, send, recv)
    row = segments[...].astype(F32)
    column = jnp.broadcast_to(row, (8, row.shape[1])).T[:, 0:1]
    penalty[...] = jnp.where(column == row, 0.0, MASKED)
    stream[...] = x[...].astype(F32)
    own_copy.wait()
    place.meet()
    clock = Clock(gather)
    clock.done = gather.begin()

    def arrived(index):
        if index > 0:
            clock.until(PARTS * index + PARTS + 3)

    saves = {}

    def save(key, src, dst, sem):
        saves[key] = pltpu.make_async_copy(src, dst, sem)
        saves[key].start()

    def saved(key):
        if key in saves:
            saves.pop(key).wait()

    for layer in range(LAYERS):
        base = 3 * layer
        arrived(base)
        loads = load_mat(whole, base, mat_c, load_sem)
        for copy in loads:
            copy.start()
        if layer > 0:
            saved("hid")
        hid[...] = stream[...].astype(BF)
        if layer > 0:
            save("hid", hid, hid_out, save_sem.at[0])
        for pair in range(2):
            loads[2 * pair].wait()
            loads[2 * pair + 1].wait()
            hidden = hid[...]
            even = nn(hidden, panel(mat_c[2 * pair, :, :, :, 0:640]))
            odd = nn(hidden, panel(mat_c[2 * pair + 1, :, :, :, 0:640]))
            for tile in range(9):
                if tile < 4:
                    value = even[:, tile * 128 : tile * 128 + 128]
                elif tile == 4:
                    value = jnp.where(low, even[:, 512:640], odd[:, 0:128])
                else:
                    value = odd[:, (tile - 4) * 128 : (tile - 4) * 128 + 128]
                group = pair * 9 + tile
                if group < 6:
                    value = (value + bias[layer, 0:1, group * 128 : group * 128 + 128]).astype(BF)
                    value = value * jnp.asarray(HEAD_DIM**-0.5, BF)
                elif group >= 12:
                    value = value + bias[layer, 1:2, (group - 12) * 128 : (group - 12) * 128 + 128]
                qkv[layer, group] = value.astype(BF)
        clock.until(clock.done + 1)
        save(("qkv", layer), qkv.at[layer], qkv_out.at[layer], save_sem.at[1 + layer])

        if layer > 0:
            saved("ctx")

        def two_heads(pair):
            slot = pair % 2

            @pl.when(pair >= 2)
            def _():
                pltpu.make_async_copy(soft.at[slot], soft_out.at[layer, pl.ds(0, 2)], soft_sem.at[0, slot]).wait()
                if layer == LAYERS - 1:
                    pltpu.make_async_copy(logit.at[slot], logits.at[pl.ds(0, 2)], soft_sem.at[1, slot]).wait()

            values = qkv[layer, 12 + pair]
            keys = qkv[layer, 6 + pair]
            if layer > 0:
                keys = jnp.concatenate([qkv[0, 6 + pair], keys], axis=1)
            for part in range(2):
                rows = pl.ds(part * 256, 256)
                parts = []
                for head in range(2):
                    mine = low if head == 0 else ~low
                    query = jnp.where(mine, qkv[layer, pair, rows, :], jnp.zeros((), BF))
                    if layer > 0:
                        before = jnp.where(mine, qkv[0, pair, rows, :], jnp.zeros((), BF))
                        query = jnp.concatenate([before, query], axis=1)
                    scores = nt(query, keys)
                    if layer == LAYERS - 1:
                        logit[slot, head, rows, :] = scores.astype(BF)
                    scores = scores + penalty[rows, :]
                    powers = jnp.exp(scores - jnp.max(scores, axis=-1, keepdims=True))
                    share = (powers * (1.0 / jnp.sum(powers, axis=-1, keepdims=True))).astype(BF)
                    soft[slot, head, rows, :] = share
                    parts.append(nn(share, values))
                ctx[pair, rows, :] = jnp.where(low, parts[0], parts[1]).astype(BF)
            pltpu.make_async_copy(
                soft.at[slot], soft_out.at[layer, pl.ds(pair * 2, 2)], soft_sem.at[0, slot]
            ).start()
            if layer == LAYERS - 1:
                pltpu.make_async_copy(logit.at[slot], logits.at[pl.ds(pair * 2, 2)], soft_sem.at[1, slot]).start()

        clock.loop(6, two_heads, 3 if layer == 0 else 2)
        for slot in range(2):
            pltpu.make_async_copy(soft.at[slot], soft_out.at[layer, pl.ds(0, 2)], soft_sem.at[0, slot]).wait()
            if layer == LAYERS - 1:
                pltpu.make_async_copy(logit.at[slot], logits.at[pl.ds(0, 2)], soft_sem.at[1, slot]).wait()
        save("ctx", ctx, ctx_out.at[layer], save_sem.at[3])

        arrived(base + 1)
        loads = load_mat(whole, base + 1, mat_u, load_sem)
        for copy in loads:
            copy.start()
        context = jnp.concatenate([ctx[pair] for pair in range(6)], axis=1)
        pieces = []
        for pair in range(2):
            even = nn(context, panel(mat_c[2 * pair, :, :, :, 512:768]))
            odd_far = nn(context, panel(mat_c[2 * pair + 1, :, :, :, 640:768]))
            odd_near = nn(context, panel(mat_c[2 * pair + 1, :, :, :, 0:128]))
            pieces += [even[:, 128:256], turn(jnp.where(low, odd_near, even[:, 0:128])), odd_far]
        first_sum = stream[...] + (jnp.concatenate(pieces, axis=1) + bias[layer, 2:3, :])
        if layer > 0:
            saved("n1")
            saved("nl")
        unit, scale = standardize(first_sum)
        n1[...] = unit
        scale_out[:, 2 * layer : 2 * layer + 1] = scale
        after = unit * gain[layer, 0:1, :] + shift[layer, 0:1, :]
        normed[...] = after
        nl[...] = after.astype(BF)
        save("n1", n1, n1_out.at[layer], save_sem.at[4])
        save("nl", nl, nl_out.at[layer], save_sem.at[5])

        if layer == 0:
            clock.until(clock.done + 1)
        if layer > 0:
            saved("act")
            saved("slope")

        def widen(n):
            wait_for(mat_u.at[n], load_sem.at[n])
            pre = nn(nl[...], panel(mat_u[n])) + up_bias[layer : layer + 1, pl.ds(pl.multiple_of(n * WIDE, WIDE), WIDE)]
            value, slant = gelu_and_slope(pre)
            act[n] = value.astype(BF)
            slope[n] = slant.astype(BF)

        clock.loop(4, widen, 2 if layer == 0 else 3)
        save("act", act, act_out.at[layer], save_sem.at[6])
        save("slope", slope, slope_out.at[layer], save_sem.at[7])
        arrived(base + 2)
        loads = [load_down(whole, base + 2, a, mat_d.at[a], load_sem.at[a]) for a in range(LINES)]
        for copies in loads:
            for copy in copies:
                copy.start()
        if layer > 0:
            saved("n2")
        n2[...] = normed[...] + bias[layer, 3:4, :]

        def narrow_down(a):
            wait_for(mat_d.at[a], load_sem.at[a])
            for b in range(2):
                n2[...] += nt(act[a, :, b * 384 : b * 384 + 384], mat_d[a, b])

        clock.loop(LINES, narrow_down, 1 if layer == 0 else 0)
        unit, scale = standardize(n2[...])
        n2[...] = unit
        scale_out[:, 2 * layer + 1 : 2 * layer + 2] = scale
        after = unit * gain[layer, 1:2, :] + shift[layer, 1:2, :]
        stream[...] = after
        save("n2", n2, n2_out.at[layer], save_sem.at[8])
    result[...] = stream[...].astype(BF)
    for key in list(saves):
        saved(key)
    clock.until(ROUNDS + 3)


def backward_kernel(
    runs, whole, x, hid2, qkv_in, ctx_in, nl_in, act_in, slope_in, n1_in, n2_in, scale_in, soft_in, out_grad, logit_grad,
    gain, *rest
):
    (grad_in, owned, vec, carry, stream, second, acc, go, go_t, nl, nl_t, unit, ctx, gctx, qkv, gqkv, ubuf, dbuf,
     actbuf, slopebuf, soft, dc_in, dc_out, load_sem, misc_sem, soft_sem, grads,
     got1, got2a, got2b, got3, got4, send, recv, free, vec_got, vec_line, vec_send, vec_recv) = rest
    place = Place(runs)
    place.greet()
    clock = Clock(Reduce(place, grads, owned, got1, got2a, got2b, got3, got4, send, recv, free))
    low = low_lanes((1, 128))
    stream[...] = out_grad[...].astype(F32)

    def copies(layer, n, slot):
        return (
            [
                pltpu.make_async_copy(whole.at[3 * layer + 1, :, :, n // 2, n % 2], ubuf.at[slot], load_sem.at[slot, 0]),
                pltpu.make_async_copy(slope_in.at[layer, n], slopebuf.at[slot], load_sem.at[slot, 2]),
            ],
            load_down(whole, 3 * layer + 2, n, dbuf.at[slot], load_sem.at[slot, 3]),
        )

    def act_copy(layer, n, slot):
        return pltpu.make_async_copy(act_in.at[layer, n], actbuf.at[slot], load_sem.at[slot, 1])

    def start_all(layer, n, slot):
        some, more = copies(layer, n, slot)
        for copy in some + more:
            copy.start()

    def wait_all(layer, n, slot):
        for copy in copies(layer, n, slot)[0]:
            copy.wait()
        wait_for(dbuf.at[slot], load_sem.at[slot, 3])

    def norm_back(layer, grad, unit, scale, row):
        vec[row[0] : row[0] + 1, :] = jnp.sum(grad * unit, axis=0, keepdims=True)
        vec[row[1] : row[1] + 1, :] = jnp.sum(grad, axis=0, keepdims=True)
        scaled = grad * gain[layer, row[2] : row[2] + 1, :]
        return (
            scaled
            - jnp.mean(scaled, axis=-1, keepdims=True)
            - unit * jnp.mean(scaled * unit, axis=-1, keepdims=True)
        ) * scale

    for layer in reversed(range(LAYERS)):
        base = 12 * layer
        early = [
            pltpu.make_async_copy(n2_in.at[layer], unit, misc_sem.at[0]),
            pltpu.make_async_copy(nl_in.at[layer], nl, misc_sem.at[1]),
            pltpu.make_async_copy(ctx_in.at[layer], ctx, misc_sem.at[2]),
            pltpu.make_async_copy(qkv_in.at[layer], qkv, misc_sem.at[3]),
        ]
        act_copy(layer, 0, 0).start()
        for copy in early:
            copy.start()
        start_all(layer, 0, 0)
        for copy in early[:2]:
            copy.wait()
        second[...] = norm_back(
            layer, stream[...], unit[...], scale_in[:, 2 * layer + 1 : 2 * layer + 2], (base + 9, base + 11, 1)
        )
        go[...] = second[...].astype(BF)
        go_t[...] = go[...].T
        nl_t[...] = nl[...].T
        late = [
            pltpu.make_async_copy(n1_in.at[layer], unit, misc_sem.at[0]),
            pltpu.make_async_copy(hid2 if layer == 1 else x, nl, misc_sem.at[1]),
        ]
        for copy in late:
            copy.start()
        vec[base + 3 : base + 4, :] = jnp.sum(go[...].astype(F32), axis=0, keepdims=True)
        acc[...] = second[...]
        if layer == 1:
            place.meet()
        clock.until(0 if layer == 1 else PARTS + 1)

        def down_grad(n):
            slot = n % 2
            act_copy(layer, n, slot).wait()

            @pl.when(n < 3)
            def _():
                act_copy(layer, n + 1, 1 - slot).start()

            for b in range(2):
                down = nn(go_t[...], actbuf[slot, :, b * 384 : b * 384 + 384]).astype(BF)
                for m in range(4):
                    for h in range(2):
                        grads[2, n, b, m // 2, m % 2, :, h * 384 : h * 384 + 384] = down[
                            192 * m + BLOCK * h : 192 * m + BLOCK * h + BLOCK, :
                        ]

        clock.loop(4, down_grad, 0 if layer == 1 else 1)
        clock.until(1 if layer == 1 else 2 * PARTS + 1)

        def chunk(n):
            slot = n % 2
            wait_all(layer, n, slot)

            @pl.when(n < 3)
            def _():
                start_all(layer, n + 1, 1 - slot)

            outer = go[...]
            wide = jnp.concatenate([nn(outer, dbuf[slot, 0]), nn(outer, dbuf[slot, 1])], axis=1)
            pre = (wide * slopebuf[slot].astype(F32)).astype(BF)
            vec[pl.ds(base + 4 + n, 1), :] = jnp.sum(pre.astype(F32), axis=0, keepdims=True)
            acc[...] += nt(pre, panel(ubuf[slot]))
            up = nn(nl_t[...], pre).astype(BF)
            grads[1, :, :, n // 2, n % 2] = up.reshape(LINES, 2, BLOCK, WIDE)

        clock.loop(4, chunk, 2 if layer == 1 else 4)

        def side_copy(n):
            return pltpu.make_async_copy(whole.at[3 * layer, :, :, n // 2, n % 2], ubuf.at[n % 2], load_sem.at[n % 2, 0])

        side_copy(0).start()
        side_copy(1).start()
        for copy in late + early[2:]:
            copy.wait()
        second[...] = norm_back(layer, acc[...], unit[...], scale_in[:, 2 * layer : 2 * layer + 1], (base + 8, base + 10, 0))
        go[...] = second[...].astype(BF)
        vec[base + 2 : base + 3, :] = jnp.sum(go[...].astype(F32), axis=0, keepdims=True)

        def tile_of(index):
            return go[:, index * 128 : index * 128 + 128]

        zero = jnp.zeros((), BF)
        outs = []
        for pair in range(2):
            mixed = turn(tile_of(3 * pair + 1).astype(F32)).astype(BF)
            outs.append((jnp.where(low, zero, mixed), tile_of(3 * pair)))
            outs.append((jnp.where(low, mixed, zero), tile_of(3 * pair + 2)))
        acc[...] = jnp.zeros_like(acc)
        for n in range(4):
            near = slice(512, 640) if n % 2 == 0 else slice(0, 128)
            side_copy(n).wait()
            acc[...] += nt(outs[n][0], panel(ubuf[n % 2, :, :, :, near])) + nt(
                outs[n][1], panel(ubuf[n % 2, :, :, :, 640:768])
            )
            side_copy((n + 2) % 4).start()
        for pair in range(6):
            gctx[pair] = acc[:, pair * 128 : pair * 128 + 128].astype(BF)

        if layer == 1:
            clock.until(PARTS + 1)
        above = logit_grad if layer == LAYERS - 1 else carry

        def fetch(pair, slot):
            return [
                pltpu.make_async_copy(soft_in.at[layer, pl.ds(pair * 2, 2)], soft.at[slot], soft_sem.at[0, slot]),
                pltpu.make_async_copy(above.at[pl.ds(pair * 2, 2)], dc_in.at[slot], soft_sem.at[1, slot]),
            ]

        for copy in fetch(0, 0):
            copy.start()

        def two_heads(pair):
            slot = pair % 2
            for copy in fetch(pair, slot):
                copy.wait()

            @pl.when(pair < 5)
            def _():
                for copy in fetch(pair + 1, 1 - slot):
                    copy.start()

            if layer > 0:

                @pl.when(pair >= 2)
                def _():
                    pltpu.make_async_copy(dc_out.at[slot], carry.at[pl.ds(0, 2)], soft_sem.at[2, slot]).wait()

            queries, keys, values, grad = qkv[pair], qkv[6 + pair], qkv[12 + pair], gctx[pair]
            both = grad.astype(F32) * ctx[pair].astype(F32)
            grad_q, grad_k, grad_v = 0.0, 0.0, 0.0
            for head in range(2):
                mine = low if head == 0 else ~low
                own = jnp.where(mine, grad, zero)
                dot = jnp.sum(jnp.where(mine, both, 0.0), axis=-1, keepdims=True)
                share = soft[slot, head]
                inner = nt(own, values)
                scores = (share.astype(F32) * (inner - dot) + dc_in[slot, head].astype(F32)).astype(BF)
                dc_out[slot, head] = scores
                grad_v = grad_v + tn(share, own)
                grad_q = grad_q + nn(scores, jnp.where(mine, keys, zero))
                grad_k = grad_k + tn(scores, jnp.where(mine, queries, zero))
            gqkv[pair] = (grad_q * HEAD_DIM**-0.5).astype(BF)
            gqkv[6 + pair] = grad_k.astype(BF)
            gqkv[12 + pair] = grad_v.astype(BF)
            if layer > 0:
                pltpu.make_async_copy(dc_out.at[slot], carry.at[pl.ds(pair * 2, 2)], soft_sem.at[2, slot]).start()

        clock.loop(6, two_heads, 2 if layer == 1 else 4)
        if layer > 0:
            for slot in range(2):
                pltpu.make_async_copy(dc_out.at[slot], carry.at[pl.ds(0, 2)], soft_sem.at[2, slot]).wait()
        for group in range(6):
            lanes = slice(group * 128, group * 128 + 128)
            vec[base : base + 1, lanes] = jnp.sum(gqkv[group].astype(F32), axis=0, keepdims=True)
            vec[base + 1 : base + 2, lanes] = jnp.sum(gqkv[12 + group].astype(F32), axis=0, keepdims=True)

        nl_t[...] = nl[...].T
        go_t[...] = jnp.concatenate([ctx[pair] for pair in range(6)], axis=1).T
        clock.until(2 * PARTS if layer == 1 else 3 * PARTS + 1)
        stream[...] = second[...]
        for n in range(4):
            pair = n // 2
            if n % 2 == 0:
                tiles = [gqkv[9 * pair + k] for k in range(4)] + [jnp.where(low, gqkv[9 * pair + 4], zero)]
            else:
                tiles = [jnp.where(low, zero, gqkv[9 * pair + 4])] + [gqkv[9 * pair + k] for k in range(5, 9)]
            side = jnp.concatenate(tiles, axis=1)
            side_copy(n).wait()
            stream[...] += nt(side, panel(ubuf[n % 2, :, :, :, 0:640]))
            if n < 2:
                side_copy(n + 2).start()
            first = nn(nl_t[...], side)
            near = nn(go_t[...], outs[n][0])
            far = nn(go_t[...], outs[n][1])
            shape = (LINES, 2, BLOCK, 128)
            mixed = 4 if n % 2 == 0 else 0
            for tile in range(5):
                value = first[:, tile * 128 : tile * 128 + 128]
                if tile == mixed:
                    value = value + near
                grads[0, :, :, n // 2, n % 2, :, tile * 128 : tile * 128 + 128] = value.astype(BF).reshape(shape)
            grads[0, :, :, n // 2, n % 2, :, 640:768] = far.astype(BF).reshape(shape)
    grad_in[...] = stream[...].astype(BF)
    clock.until(ROUNDS + GAP)
    steps = [place.at(c=1 - place.c), place.at(y=1 - place.y), place.at(b=1 - place.b)]
    for k, to in enumerate(steps):
        push(vec, vec_got.at[k], vec_send.at[k], vec_recv.at[k], to)
        clock.until(ROUNDS + GAP + k + 1)
        wait_for(vec, vec_send.at[k])
        wait_for(vec_got.at[k], vec_recv.at[k])
        vec[...] += vec_got[k]
    for o in range(1, LINES):
        push(vec, vec_line.at[place.a], vec_send.at[3], vec_recv.at[3], place.at(a=(place.a + o) % LINES))
    clock.until(ROUNDS + GAP + 4)
    wait_for(vec_line.at[pl.ds(0, LINES - 1)], vec_send.at[3])
    wait_for(vec_line.at[pl.ds(0, LINES - 1)], vec_recv.at[3])
    vec_line[place.a] = vec[...]
    vec[...] = (vec_line[0] + vec_line[1]) + (vec_line[2] + vec_line[3])


def forward(runs, mats, x, segments, bias, up_bias, gain, shift):
    length, width = x.shape
    heads = width // HEAD_DIM
    sds = jax.ShapeDtypeStruct
    vmem, hbm = pl.BlockSpec(memory_space=pltpu.VMEM), pl.BlockSpec(memory_space=pltpu.HBM)
    outs = [
        (sds((length, width), BF), vmem),
        (sds((heads, length, length), BF), hbm),
        (sds((LAYERS, heads, length, length), BF), hbm),
        (sds((LAYERS, 18, length, 128), BF), hbm),
        (sds((LAYERS, 6, length, 128), BF), hbm),
        (sds((length, width), BF), hbm),
        (sds((LAYERS, length, width), BF), hbm),
        (sds((LAYERS, 4, length, width), BF), hbm),
        (sds((LAYERS, 4, length, width), BF), hbm),
        (sds((LAYERS, length, width), F32), hbm),
        (sds((LAYERS, length, width), F32), hbm),
        (sds((length, 2 * LAYERS), F32), vmem),
    ]
    outs.append((sds((6, LINES, 2, 2, 2, BLOCK, WIDE), BF), hbm))
    dma = pltpu.SemaphoreType.DMA
    scratch = [
        pltpu.VMEM((length, width), F32),
        pltpu.VMEM((LAYERS, 18, length, 128), BF),
        pltpu.VMEM((6, length, 128), BF),
        pltpu.VMEM((length, width), F32),
        pltpu.VMEM((length, width), F32),
        pltpu.VMEM((length, width), F32),
        pltpu.VMEM((length, width), BF),
        pltpu.VMEM((length, width), BF),
        pltpu.VMEM((4, length, width), BF),
        pltpu.VMEM((4, length, width), BF),
        pltpu.VMEM((length, length), F32),
        pltpu.VMEM((2, 2, length, length), BF),
        pltpu.VMEM((2, 2, length, length), BF),
        pltpu.VMEM((4, LINES, 2, BLOCK, WIDE), BF),
        pltpu.VMEM((4, LINES, 2, BLOCK, WIDE), BF),
        pltpu.VMEM((LINES, 2, WIDE, 384), BF),
        dma((4,)),
        dma((2, 2)),
        dma((9,)),
        dma(()),
        dma((ROUNDS, 2, 4)),
        dma((ROUNDS, 2, 7)),
        pltpu.VMEM((6, BLOCK, WIDE), BF),
        pltpu.VMEM((BLOCK, 640), F32),
        pltpu.VMEM((BLOCK, 256), F32),
    ]
    return pl.pallas_call(
        functools.partial(forward_kernel, runs),
        out_shape=[o[0] for o in outs],
        in_specs=[vmem] * 10,
        out_specs=[o[1] for o in outs],
        scratch_shapes=scratch,
        compiler_params=pltpu.CompilerParams(vmem_limit_bytes=60 << 20, collective_id=0, has_side_effects=True),
        name="ahead",
    )(*mats, x, segments, bias, up_bias, gain, shift)


def backward(runs, whole, x, kept, out_grad, logit_grad, gain):
    soft, qkv, ctx, hid2, nl, act, slope, n1, n2, scale = kept
    length, width = x.shape
    heads = width // HEAD_DIM
    sds = jax.ShapeDtypeStruct
    vmem, hbm = pl.BlockSpec(memory_space=pltpu.VMEM), pl.BlockSpec(memory_space=pltpu.HBM)
    blocks = (LINES, 2, 2, 2, BLOCK, WIDE)
    outs = [
        (sds((length, width), BF), vmem),
        (sds((6, BLOCK, WIDE), F32), vmem),
        (sds((12 * LAYERS, width), F32), vmem),
        (sds((heads, length, length), BF), hbm),
    ]
    dma = pltpu.SemaphoreType.DMA
    scratch = [
        pltpu.VMEM((length, width), F32),
        pltpu.VMEM((length, width), F32),
        pltpu.VMEM((length, width), F32),
        pltpu.VMEM((length, width), BF),
        pltpu.VMEM((width, length), BF),
        pltpu.VMEM((length, width), BF),
        pltpu.VMEM((width, length), BF),
        pltpu.VMEM((length, width), F32),
        pltpu.VMEM((6, length, 128), BF),
        pltpu.VMEM((6, length, 128), BF),
        pltpu.VMEM((18, length, 128), BF),
        pltpu.VMEM((18, length, 128), BF),
        pltpu.VMEM((2, LINES, 2, BLOCK, WIDE), BF),
        pltpu.VMEM((2, 2, WIDE, 384), BF),
        pltpu.VMEM((2, length, width), BF),
        pltpu.VMEM((2, length, width), BF),
        pltpu.VMEM((2, 2, length, length), BF),
        pltpu.VMEM((2, 2, length, length), BF),
        pltpu.VMEM((2, 2, length, length), BF),
        dma((2, 4)),
        dma((4,)),
        dma((3, 2)),
        pltpu.VMEM((3,) + blocks, BF),
        pltpu.VMEM((SETS, 2, 2, LINES, 2, PIECE, WIDE), BF),
        pltpu.VMEM((SETS, LINES, 2, PIECE, WIDE), BF),
        pltpu.VMEM((SETS, 2, LINES, PIECE, WIDE), BF),
        pltpu.VMEM((SETS, 2, LINES, PIECE, WIDE), BF),
        pltpu.VMEM((SETS, 2, LINES - 1, PIECE, WIDE), BF),
        dma((SETS, 2, 4)),
        dma((SETS, 2, 4)),
        pltpu.SemaphoreType.REGULAR((SETS,)),
        pltpu.VMEM((3, 12 * LAYERS, width), F32),
        pltpu.VMEM((LINES, 12 * LAYERS, width), F32),
        dma((4,)),
        dma((4,)),
    ]
    return pl.pallas_call(
        functools.partial(backward_kernel, runs),
        out_shape=[o[0] for o in outs],
        in_specs=[hbm] * 10 + [vmem, hbm, vmem, hbm, vmem],
        out_specs=[o[1] for o in outs],
        scratch_shapes=scratch,
        compiler_params=pltpu.CompilerParams(vmem_limit_bytes=62 << 20, collective_id=1, has_side_effects=True),
        name="back",
    )(whole, x, hid2, qkv, ctx, nl, act, slope, n1, n2, scale, soft, out_grad, logit_grad, gain)


def finish_kernel(owned, vec, result_in, grad_in, logits_in, result, logits, grad, g_qkv, g_out, g_up, g_down,
                  g_bias, g_up_bias, g_gain, g_shift, stage, sem):
    heads = logits.shape[0]
    count = stage.shape[0]
    step = heads // count
    parts = [pl.ds(k * step, step) for k in range(count)]
    for k, at in enumerate(parts):
        pltpu.make_async_copy(logits_in.at[at], stage.at[k], sem.at[0, k]).start()
    result[...] = result_in[...]
    grad[...] = grad_in[...]
    odd = lax.broadcasted_iota(jnp.int32, (1, 128), 1) * 0 + lax.axis_index("narrow") % 2 == 1
    low = low_lanes((1, 128))
    for layer in range(LAYERS):
        block = owned[3 * layer]
        moved = pltpu.roll(block, WIDE - HEAD_DIM, 1)
        for k in range(5):
            lanes = slice(k * 128, min(k * 128 + 128, 576))
            tile = slice(k * 128, k * 128 + 128)
            g_qkv[layer, :, lanes] = jnp.where(odd, moved[:, tile], block[:, tile])[:, : lanes.stop - lanes.start]
        last = block[:, 640:768]
        g_out[layer, :, 0:128] = jnp.where(odd, jnp.where(low, block[:, 0:128], turn(last)), last)
        g_out[layer, :, 128:192] = jnp.where(odd, turn(last), turn(block[:, 512:640]))[:, 0:64]
        g_up[layer] = owned[3 * layer + 1]
        down = owned[3 * layer + 2]
        g_down[layer, 0:BLOCK, :] = down[:, 0:384]
        g_down[layer, BLOCK : 2 * BLOCK, :] = down[:, 384:768]
        base = 12 * layer
        g_bias[layer] = vec[base : base + 4, :]
        for n in range(4):
            g_up_bias[layer : layer + 1, n * WIDE : n * WIDE + WIDE] = vec[base + 4 + n : base + 5 + n, :]
        g_gain[layer] = vec[base + 8 : base + 10, :]
        g_shift[layer] = vec[base + 10 : base + 12, :]
    for k, at in enumerate(parts):
        pltpu.make_async_copy(logits_in.at[at], stage.at[k], sem.at[0, k]).wait()
        pltpu.make_async_copy(stage.at[k], logits.at[at], sem.at[1, k]).start()
    for k, at in enumerate(parts):
        pltpu.make_async_copy(stage.at[k], logits.at[at], sem.at[1, k]).wait()


def finish(owned, vec, result, grad, logits):
    sds = jax.ShapeDtypeStruct
    vmem, hbm = pl.BlockSpec(memory_space=pltpu.VMEM), pl.BlockSpec(memory_space=pltpu.HBM)
    heads, length, _ = logits.shape
    outs = [
        (sds(result.shape, BF), vmem),
        (sds(logits.shape, BF), hbm),
        (sds(grad.shape, BF), vmem),
        (sds((LAYERS, BLOCK, 576), F32), vmem),
        (sds((LAYERS, BLOCK, 192), F32), vmem),
        (sds((LAYERS, BLOCK, WIDE), F32), vmem),
        (sds((LAYERS, 2 * BLOCK, 384), F32), vmem),
        (sds((LAYERS, 4, WIDE), F32), vmem),
        (sds((LAYERS, 4 * WIDE), F32), vmem),
        (sds((LAYERS, 2, WIDE), F32), vmem),
        (sds((LAYERS, 2, WIDE), F32), vmem),
    ]
    return pl.pallas_call(
        finish_kernel,
        out_shape=[o[0] for o in outs],
        in_specs=[vmem] * 4 + [hbm],
        out_specs=[o[1] for o in outs],
        scratch_shapes=[pltpu.VMEM((6, heads // 6, length, length), BF), pltpu.SemaphoreType.DMA((2, 6))],
        compiler_params=pltpu.CompilerParams(vmem_limit_bytes=48 << 20),
        name="finish",
    )(owned, vec, result, grad, logits)


def body(runs, inputs, segments, out_grad, logit_grad, w_qkv, w_out, w_up, w_down, biases, up_bias, gains, shifts):
    mats = [w_qkv, w_out, w_up, w_down]
    groups = [[g * runs + r for r in range(runs)] for g in range(2 * LINES)]
    if runs > 1:
        mats = [lax.all_gather(w.astype(BF), "dp", axis_index_groups=groups, axis=1, tiled=True) for w in mats]
    result, logits, *kept, whole = forward(runs, mats[:3] + [jnp.swapaxes(mats[3], 1, 2)], inputs[0], segments, biases, up_bias, gains, shifts)
    grad_in, owned, vec, _ = backward(runs, whole, inputs[0], kept, out_grad[0], logit_grad[0], gains)
    result, logits, grad_in, *grads = finish(owned, vec, result, grad_in, logits)
    grads[3] = jnp.swapaxes(grads[3], 1, 2)
    if runs > 1:
        grads = [
            lax.psum_scatter(g, "dp", axis_index_groups=groups, scatter_dimension=1, tiled=True) for g in grads[:4]
        ] + list(lax.psum(tuple(grads[4:]), "dp", axis_index_groups=groups))
    return (result[None], logits[None], grad_in[None], *grads)


def solution(mesh):
    rows = P(("dp", "narrow"), None, None)
    heads = P(("dp", "narrow"), None, None, None)
    blocks = P(None, "dp", "narrow")
    runs = mesh.shape["dp"] // (2 * LINES)
    return jax.shard_map(
        functools.partial(body, runs),
        mesh=mesh,
        in_specs=(rows, P(("dp", "narrow"), None), rows, heads) + (blocks,) * 4 + (P(),) * 4,
        out_specs=(rows, heads, rows) + (blocks,) * 4 + (P(),) * 4,
        check_vma=False,
    )
```

```python
import functools

import jax
import jax.numpy as jnp
from jax import lax
import jax.experimental.pallas as pl
import jax.experimental.pallas.tpu as pltpu
from jax.sharding import PartitionSpec as P

BF, F32 = jnp.bfloat16, jnp.float32
MESH = pl.DeviceIdType.MESH
HEAD_DIM = 64
LAYERS = 2
EPS = 1e-6
MASKED = -1e30

LINES = 4
BLOCK = 96
HALF = BLOCK // 2
WIDE = 768
PARTS = 3
PIECE = HALF // PARTS
ROUNDS = 6 * PARTS
AHEAD = 4
GAP = 0
SETS = 6


def nn(left, right):
    return lax.dot_general(left, right, (((1,), (0,)), ((), ())), preferred_element_type=F32)


def nt(left, right):
    return lax.dot_general(left, right, (((1,), (1,)), ((), ())), preferred_element_type=F32)


def tn(left, right):
    return lax.dot_general(left, right, (((0,), (0,)), ((), ())), preferred_element_type=F32)


def low_lanes(shape):
    return lax.broadcasted_iota(jnp.int32, shape, len(shape) - 1) % 128 < HEAD_DIM


def turn(tile):
    return pltpu.roll(tile, HEAD_DIM, 1)


class Place:
    def __init__(self, runs):
        d, n = lax.axis_index("dp"), lax.axis_index("narrow")
        self.runs, self.run = runs, d % runs
        self.a, self.b, self.y, self.c = d // runs // 2, d // runs % 2, n // 2, n % 2

    def at(self, a=None, b=None, y=None, c=None):
        a = self.a if a is None else a
        b = self.b if b is None else b
        y = self.y if y is None else y
        c = self.c if c is None else c
        return ((a * 2 + b) * self.runs + self.run, y * 2 + c)

    def peers(self):
        lines = [self.at(a=(self.a + o) % LINES) for o in range(1, LINES)]
        return lines + [self.at(b=1 - self.b), self.at(y=1 - self.y), self.at(c=1 - self.c)]

    def greet(self):
        for peer in self.peers():
            pl.semaphore_signal(pltpu.get_barrier_semaphore(), inc=1, device_id=peer, device_id_type=MESH)

    def meet(self):
        pl.semaphore_wait(pltpu.get_barrier_semaphore(), len(self.peers()))


def push(src, dst, send, recv, to):
    pltpu.make_async_remote_copy(
        src_ref=src, dst_ref=dst, send_sem=send, recv_sem=recv, device_id=to, device_id_type=MESH
    ).start()


def wait_for(view, sem):
    pltpu.make_async_copy(view, view, sem).wait()


class Gather:
    def __init__(self, place, whole, send, recv):
        self.p, self.whole, self.send, self.recv = place, whole, send, recv

    def rows(self, t, half):
        return pl.ds(pl.multiple_of(half * HALF + (t % PARTS) * PIECE, 16), PIECE)

    def line(self, t, half, b, y, c):
        return self.whole.at[t // PARTS, :, b, y, c, self.rows(t, half), :]

    def stage1(self, t):
        p = self.p
        for half in range(2):
            mine = self.whole.at[t // PARTS, p.a, p.b, p.y, p.c, self.rows(t, half), :]
            for o in range(1, LINES):
                push(mine, mine, self.send.at[t, half, 0], self.recv.at[t, half, 0], p.at(a=(p.a + o) % LINES))

    def first(self, half):
        p = self.p
        return (1 - p.b, p.y) if half == 0 else (p.b, 1 - p.y)

    def second(self, half):
        p = self.p
        return (p.b, 1 - p.y) if half == 0 else (1 - p.b, p.y)

    def stage2(self, t):
        p = self.p
        for half in range(2):
            some = self.whole.at[t // PARTS, pl.ds(0, LINES - 1), 0, 0, 0, self.rows(t, half), :]
            wait_for(some, self.recv.at[t, half, 0])
            line = self.line(t, half, p.b, p.y, p.c)
            b1, y1 = self.first(half)
            b2, y2 = self.second(half)
            push(line, line, self.send.at[t, half, 1], self.recv.at[t, half, 1], p.at(b=b1, y=y1))
            push(line, line, self.send.at[t, half, 2], self.recv.at[t, half, 2], p.at(b=b2, y=y2))
            push(line, line, self.send.at[t, half, 3], self.recv.at[t, half, 4], p.at(c=1 - p.c))

    def stage3(self, t):
        p = self.p
        for half in range(2):
            b1, y1 = self.first(half)
            b2, y2 = self.second(half)
            line = self.line(t, half, b1, y1, p.c)
            wait_for(line, self.recv.at[t, half, 1])
            push(line, line, self.send.at[t, half, 2], self.recv.at[t, half, 3], p.at(b=b2, y=y2))
            push(line, line, self.send.at[t, half, 3], self.recv.at[t, half, 5], p.at(c=1 - p.c))

    def stage4(self, t):
        p = self.p
        for half in range(2):
            b2, y2 = self.second(half)
            far = self.line(t, half, b2, y2, p.c)
            wait_for(far, self.recv.at[t, half, 2])
            push(far, far, self.send.at[t, half, 3], self.recv.at[t, half, 6], p.at(c=1 - p.c))
            far = self.line(t, half, 1 - p.b, 1 - p.y, p.c)
            wait_for(far, self.recv.at[t, half, 3])
            push(far, far, self.send.at[t, half, 3], self.recv.at[t, half, 6], p.at(c=1 - p.c))

    def stage5(self, t):
        for half in range(2):
            line = self.line(t, half, 0, 0, 0)
            wait_for(line, self.recv.at[t, half, 4])
            wait_for(line, self.recv.at[t, half, 5])
            two = self.whole.at[t // PARTS, :, :, 0, 0, self.rows(t, half), :]
            wait_for(two, self.recv.at[t, half, 6])
            some = self.whole.at[t // PARTS, pl.ds(0, LINES - 1), 0, 0, 0, self.rows(t, half), :]
            wait_for(some, self.send.at[t, half, 0])
            wait_for(line, self.send.at[t, half, 1])
            wait_for(two, self.send.at[t, half, 2])
            four = self.whole.at[t // PARTS, :, :, :, 0, self.rows(t, half), :]
            wait_for(four, self.send.at[t, half, 3])

    def round(self, t):
        @pl.when(t < ROUNDS)
        def _():
            self.stage2(t)

        @pl.when(t + AHEAD < ROUNDS)
        def _():
            self.stage1(t + AHEAD)

        @pl.when((t >= 1) & (t - 1 < ROUNDS))
        def _():
            self.stage3(t - 1)

        @pl.when((t >= 2 + PARTS) & (t - 2 < ROUNDS))
        def _():
            self.stage4(t - 2)

        @pl.when((t >= 3 + PARTS) & (t - 3 < ROUNDS))
        def _():
            self.stage5(t - 3)

    def begin(self):
        def loop(start, stop, stage):
            def step(t, _):
                stage(t)
                return 0

            lax.fori_loop(start, stop, step, 0)

        loop(0, PARTS, self.stage1)
        loop(0, PARTS, self.stage2)
        loop(PARTS, PARTS + 1 + AHEAD, self.stage1)
        loop(0, PARTS, self.stage3)
        self.stage2(PARTS)
        loop(0, PARTS, self.stage4)
        loop(0, PARTS, self.stage5)
        return PARTS + 1


class Reduce:
    def __init__(self, place, grads, owned, got1, got2a, got2b, got3, got4, send, recv, free):
        self.p, self.grads, self.owned = place, grads, owned
        self.got1, self.got2, self.got3, self.got4 = got1, (got2a, got2b), got3, got4
        self.send, self.recv, self.free = send, recv, free

    def rows(self, t, half):
        return pl.ds(pl.multiple_of(half * HALF + (t % PARTS) * PIECE, 16), PIECE)

    def mat(self, t):
        return 2 - (t // PARTS) % 3

    def stage1(self, t):
        p, s = self.p, t % SETS

        @pl.when(t >= SETS)
        def _():
            pl.semaphore_wait(self.free.at[s], LINES + 2)

        for half in range(2):
            for y in range(2):
                push(
                    self.grads.at[self.mat(t), :, :, y, 1 - p.c, self.rows(t, half), :],
                    self.got1.at[s, half, y],
                    self.send.at[s, half, 0],
                    self.recv.at[s, half, 0],
                    p.at(c=1 - p.c),
                )

    def stage2(self, t):
        p, s = self.p, t % SETS
        for half in range(2):
            wait_for(self.got1.at[s, half], self.recv.at[s, half, 0])
            rows = self.rows(t, half)
            for y in range(2):
                self.got1[s, half, y] = self.got1[s, half, y] + self.grads[self.mat(t), :, :, y, p.c, rows, :]
            if half == 0:
                push(
                    self.got1.at[s, half, 1 - p.y],
                    self.got2[0].at[s],
                    self.send.at[s, half, 1],
                    self.recv.at[s, half, 1],
                    p.at(y=1 - p.y),
                )
            else:
                push(
                    self.got1.at[s, half, :, :, 1 - p.b],
                    self.got2[1].at[s],
                    self.send.at[s, half, 1],
                    self.recv.at[s, half, 1],
                    p.at(b=1 - p.b),
                )
        for half in range(2):
            wait_for(self.got1.at[s, half], self.send.at[s, half, 0])

    def stage3(self, t):
        p, s = self.p, t % SETS
        for half in range(2):
            got = self.got2[half]
            wait_for(got.at[s], self.recv.at[s, half, 1])
            if half == 0:
                got[s] = got[s] + self.got1[s, half, p.y]
                src, to = got.at[s, :, 1 - p.b], p.at(b=1 - p.b)
            else:
                got[s] = got[s] + self.got1[s, half, :, :, p.b]
                src, to = got.at[s, 1 - p.y], p.at(y=1 - p.y)
            push(src, self.got3.at[s, half], self.send.at[s, half, 2], self.recv.at[s, half, 2], to)

    def stage4(self, t):
        p, s = self.p, t % SETS
        for half in range(2):
            wait_for(self.got3.at[s, half], self.recv.at[s, half, 2])
            mine = self.got2[0][s, :, p.b] if half == 0 else self.got2[1][s, p.y]
            self.got3[s, half] = self.got3[s, half] + mine
            for o in range(1, LINES):
                a = (p.a + o) % LINES
                push(
                    self.got3.at[s, half, a],
                    self.got4.at[s, half, o - 1],
                    self.send.at[s, half, 3],
                    self.recv.at[s, half, 3],
                    p.at(a=a),
                )

    def stage5(self, t):
        p, s = self.p, t % SETS
        for half in range(2):
            wait_for(self.got4.at[s, half], self.recv.at[s, half, 3])
            total = self.got3[s, half, p.a].astype(F32)
            for o in range(LINES - 1):
                total = total + self.got4[s, half, o].astype(F32)
            self.owned[5 - t // PARTS, self.rows(t, half), :] = total
            wait_for(self.got2[half].at[s], self.send.at[s, half, 1])
            wait_for(self.got3.at[s, half], self.send.at[s, half, 2])
            wait_for(self.got4.at[s, half], self.send.at[s, half, 3])

        @pl.when(t + SETS < ROUNDS)
        def _():
            for peer in p.peers():
                pl.semaphore_signal(self.free.at[s], inc=1, device_id=peer, device_id_type=MESH)

    def round(self, v):
        last = ROUNDS - PARTS
        for lag, stage in enumerate((self.stage1, self.stage2, self.stage3, self.stage4, self.stage5)):
            t = v - lag

            @pl.when((t >= 0) & (t < last))
            def _(stage=stage, t=t):
                stage(t)

            @pl.when((t >= last + GAP) & (t < ROUNDS + GAP))
            def _(stage=stage, t=t):
                stage(t - GAP)


class Clock:
    def __init__(self, transfer):
        self.transfer, self.done = transfer, 0

    def until(self, count):
        if count > self.done:

            def step(t, _):
                self.transfer.round(t)
                return 0

            lax.fori_loop(self.done, count, step, 0)
            self.done = count

    def loop(self, count, work, rounds):
        start = self.done

        def step(i, _):
            work(i)
            if rounds > 0:

                @pl.when(((i + 1) * rounds) // count > (i * rounds) // count)
                def _():
                    self.transfer.round(start + (i * rounds) // count)

            return 0

        lax.fori_loop(0, count, step, 0)
        self.done = start + rounds


def gelu_and_slope(values):
    size = jnp.abs(values)
    below = 1.0 + (0.3275911 * 0.7071067811865476) * size
    rough = pl.reciprocal(below, approx=True)
    t = rough * (2.0 - below * rough)
    bell = jnp.exp(-0.5 * values * values)
    poly = t * (
        0.5 * 0.254829592
        + t * (0.5 * -0.284496736 + t * (0.5 * 1.421413741 + t * (0.5 * -1.453152027 + t * (0.5 * 1.061405429))))
    )
    tail = poly * bell
    phi = jnp.where(values < 0, tail, 1.0 - tail)
    return values * phi, phi + values * (bell * 0.3989422804014327)


def standardize(values):
    centred = values - jnp.mean(values, axis=-1, keepdims=True)
    scale = lax.rsqrt(jnp.mean(centred * centred, axis=-1, keepdims=True) + EPS)
    return centred * scale, scale


def load_mat(whole, index, buffer, sem):
    return [
        pltpu.make_async_copy(whole.at[index, :, :, n // 2, n % 2], buffer.at[n], sem.at[n]) for n in range(4)
    ]


def load_down(whole, index, a, buffer, sem):
    out = []
    for n in range(4):
        for h in range(2):
            src = whole.at[index, a, :, n // 2, n % 2, :, pl.ds(h * 384, 384)]
            out.append(pltpu.make_async_copy(src, buffer.at[:, pl.ds(192 * n + BLOCK * h, BLOCK), :], sem))
    return out


def panel(block):
    return block.reshape(WIDE, block.shape[-1])


def forward_kernel(
    runs, w_qkv, w_out, w_up, w_down, x, segments, bias, up_bias, gain, shift,
    result, logits, soft_out, qkv_out, ctx_out, hid_out, nl_out, act_out, slope_out, n1_out, n2_out, scale_out, *rest
):
    (whole, stream, qkv, ctx, normed, n1, n2, nl, hid, act, slope, penalty, soft, logit, mat_c, mat_u, mat_d,
     load_sem, soft_sem, save_sem, own_sem, send, recv, own, pad_qkv, pad_out) = rest
    place = Place(runs)
    place.greet()
    odd = lax.broadcasted_iota(jnp.int32, (1, 128), 1) * 0 + place.c == 1
    low = low_lanes((1, 128))
    for layer in range(LAYERS):
        pad_qkv[:, 0:576] = w_qkv[layer].astype(F32)
        pad_out[:, 0:192] = w_out[layer].astype(F32)
        plain = pad_qkv[...]
        moved = pltpu.roll(plain, HEAD_DIM, 1)
        near, far = pad_out[:, 0:128], pad_out[:, 128:256]
        tiles = [(plain[:, k * 128 : k * 128 + 128], moved[:, k * 128 : k * 128 + 128]) for k in range(5)]
        tiles[4] = (jnp.where(low, tiles[4][0], turn(far)), tiles[4][1])
        tiles[0] = (tiles[0][0], jnp.where(low, near, tiles[0][1]))
        tiles.append((near, jnp.where(low, turn(near), turn(far))))
        for k, (even_form, odd_form) in enumerate(tiles):
            own[3 * layer, :, k * 128 : k * 128 + 128] = jnp.where(odd, odd_form, even_form).astype(BF)
        own[3 * layer + 1] = w_up[layer].astype(BF)
        own[3 * layer + 2, :, 0:384] = w_down[layer, 0:BLOCK, :].astype(BF)
        own[3 * layer + 2, :, 384:768] = w_down[layer, BLOCK : 2 * BLOCK, :].astype(BF)
    own_copy = pltpu.make_async_copy(own, whole.at[:, place.a, place.b, place.y, place.c], own_sem)
    own_copy.start()
    gather = Gather(place, whole, send, recv)
    row = segments[...].astype(F32)
    column = jnp.broadcast_to(row, (8, row.shape[1])).T[:, 0:1]
    penalty[...] = jnp.where(column == row, 0.0, MASKED)
    stream[...] = x[...].astype(F32)
    own_copy.wait()
    place.meet()
    clock = Clock(gather)
    clock.done = gather.begin()

    def arrived(index):
        if index > 0:
            clock.until(PARTS * index + PARTS + 3)

    saves = {}

    def save(key, src, dst, sem):
        saves[key] = pltpu.make_async_copy(src, dst, sem)
        saves[key].start()

    def saved(key):
        if key in saves:
            saves.pop(key).wait()

    for layer in range(LAYERS):
        base = 3 * layer
        arrived(base)
        loads = load_mat(whole, base, mat_c, load_sem)
        for copy in loads:
            copy.start()
        if layer > 0:
            saved("hid")
        hid[...] = stream[...].astype(BF)
        if layer > 0:
            save("hid", hid, hid_out, save_sem.at[0])
        for pair in range(2):
            loads[2 * pair].wait()
            loads[2 * pair + 1].wait()
            hidden = hid[...]
            even = nn(hidden, panel(mat_c[2 * pair, :, :, :, 0:640]))
            odd = nn(hidden, panel(mat_c[2 * pair + 1, :, :, :, 0:640]))
            for tile in range(9):
                if tile < 4:
                    value = even[:, tile * 128 : tile * 128 + 128]
                elif tile == 4:
                    value = jnp.where(low, even[:, 512:640], odd[:, 0:128])
                else:
                    value = odd[:, (tile - 4) * 128 : (tile - 4) * 128 + 128]
                group = pair * 9 + tile
                if group < 6:
                    value = (value + bias[layer, 0:1, group * 128 : group * 128 + 128]).astype(BF)
                    value = value * jnp.asarray(HEAD_DIM**-0.5, BF)
                elif group >= 12:
                    value = value + bias[layer, 1:2, (group - 12) * 128 : (group - 12) * 128 + 128]
                qkv[layer, group] = value.astype(BF)
        clock.until(clock.done + 1)
        save(("qkv", layer), qkv.at[layer], qkv_out.at[layer], save_sem.at[1 + layer])

        if layer > 0:
            saved("ctx")

        def two_heads(pair):
            slot = pair % 2

            @pl.when(pair >= 2)
            def _():
                pltpu.make_async_copy(soft.at[slot], soft_out.at[layer, pl.ds(0, 2)], soft_sem.at[0, slot]).wait()
                if layer == LAYERS - 1:
                    pltpu.make_async_copy(logit.at[slot], logits.at[pl.ds(0, 2)], soft_sem.at[1, slot]).wait()

            values = qkv[layer, 12 + pair]
            keys = qkv[layer, 6 + pair]
            if layer > 0:
                keys = jnp.concatenate([qkv[0, 6 + pair], keys], axis=1)
            for part in range(2):
                rows = pl.ds(part * 256, 256)
                parts = []
                for head in range(2):
                    mine = low if head == 0 else ~low
                    query = jnp.where(mine, qkv[layer, pair, rows, :], jnp.zeros((), BF))
                    if layer > 0:
                        before = jnp.where(mine, qkv[0, pair, rows, :], jnp.zeros((), BF))
                        query = jnp.concatenate([before, query], axis=1)
                    scores = nt(query, keys)
                    if layer == LAYERS - 1:
                        logit[slot, head, rows, :] = scores.astype(BF)
                    scores = scores + penalty[rows, :]
                    powers = jnp.exp(scores - jnp.max(scores, axis=-1, keepdims=True))
                    share = (powers * (1.0 / jnp.sum(powers, axis=-1, keepdims=True))).astype(BF)
                    soft[slot, head, rows, :] = share
                    parts.append(nn(share, values))
                ctx[pair, rows, :] = jnp.where(low, parts[0], parts[1]).astype(BF)
            pltpu.make_async_copy(
                soft.at[slot], soft_out.at[layer, pl.ds(pair * 2, 2)], soft_sem.at[0, slot]
            ).start()
            if layer == LAYERS - 1:
                pltpu.make_async_copy(logit.at[slot], logits.at[pl.ds(pair * 2, 2)], soft_sem.at[1, slot]).start()

        clock.loop(6, two_heads, 3 if layer == 0 else 2)
        for slot in range(2):
            pltpu.make_async_copy(soft.at[slot], soft_out.at[layer, pl.ds(0, 2)], soft_sem.at[0, slot]).wait()
            if layer == LAYERS - 1:
                pltpu.make_async_copy(logit.at[slot], logits.at[pl.ds(0, 2)], soft_sem.at[1, slot]).wait()
        save("ctx", ctx, ctx_out.at[layer], save_sem.at[3])

        arrived(base + 1)
        loads = load_mat(whole, base + 1, mat_u, load_sem)
        for copy in loads:
            copy.start()
        context = jnp.concatenate([ctx[pair] for pair in range(6)], axis=1)
        pieces = []
        for pair in range(2):
            even = nn(context, panel(mat_c[2 * pair, :, :, :, 512:768]))
            odd_far = nn(context, panel(mat_c[2 * pair + 1, :, :, :, 640:768]))
            odd_near = nn(context, panel(mat_c[2 * pair + 1, :, :, :, 0:128]))
            pieces += [even[:, 128:256], turn(jnp.where(low, odd_near, even[:, 0:128])), odd_far]
        first_sum = stream[...] + (jnp.concatenate(pieces, axis=1) + bias[layer, 2:3, :])
        if layer > 0:
            saved("n1")
            saved("nl")
        unit, scale = standardize(first_sum)
        n1[...] = unit
        scale_out[:, 2 * layer : 2 * layer + 1] = scale
        after = unit * gain[layer, 0:1, :] + shift[layer, 0:1, :]
        normed[...] = after
        nl[...] = after.astype(BF)
        save("n1", n1, n1_out.at[layer], save_sem.at[4])
        save("nl", nl, nl_out.at[layer], save_sem.at[5])

        if layer == 0:
            clock.until(clock.done + 1)
        if layer > 0:
            saved("act")
            saved("slope")

        def widen(n):
            wait_for(mat_u.at[n], load_sem.at[n])
            pre = nn(nl[...], panel(mat_u[n])) + up_bias[layer : layer + 1, pl.ds(pl.multiple_of(n * WIDE, WIDE), WIDE)]
            value, slant = gelu_and_slope(pre)
            act[n] = value.astype(BF)
            slope[n] = slant.astype(BF)

        clock.loop(4, widen, 2 if layer == 0 else 3)
        save("act", act, act_out.at[layer], save_sem.at[6])
        save("slope", slope, slope_out.at[layer], save_sem.at[7])
        arrived(base + 2)
        loads = [load_down(whole, base + 2, a, mat_d.at[a], load_sem.at[a]) for a in range(LINES)]
        for copies in loads:
            for copy in copies:
                copy.start()
        if layer > 0:
            saved("n2")
        n2[...] = normed[...] + bias[layer, 3:4, :]

        def narrow_down(a):
            wait_for(mat_d.at[a], load_sem.at[a])
            for b in range(2):
                n2[...] += nt(act[a, :, b * 384 : b * 384 + 384], mat_d[a, b])

        clock.loop(LINES, narrow_down, 1 if layer == 0 else 0)
        unit, scale = standardize(n2[...])
        n2[...] = unit
        scale_out[:, 2 * layer + 1 : 2 * layer + 2] = scale
        after = unit * gain[layer, 1:2, :] + shift[layer, 1:2, :]
        stream[...] = after
        save("n2", n2, n2_out.at[layer], save_sem.at[8])
    result[...] = stream[...].astype(BF)
    for key in list(saves):
        saved(key)
    clock.until(ROUNDS + 3)


def backward_kernel(
    runs, whole, x, hid2, qkv_in, ctx_in, nl_in, act_in, slope_in, n1_in, n2_in, scale_in, soft_in, out_grad, logit_grad,
    gain, *rest
):
    (grad_in, owned, vec, carry, stream, second, acc, go, go_t, nl, nl_t, unit, ctx, gctx, qkv, gqkv, ubuf, dbuf,
     actbuf, slopebuf, soft, dc_in, dc_out, load_sem, misc_sem, soft_sem, grads,
     got1, got2a, got2b, got3, got4, send, recv, free, vec_got, vec_line, vec_send, vec_recv) = rest
    place = Place(runs)
    place.greet()
    clock = Clock(Reduce(place, grads, owned, got1, got2a, got2b, got3, got4, send, recv, free))
    low = low_lanes((1, 128))
    stream[...] = out_grad[...].astype(F32)

    def copies(layer, n, slot):
        return (
            [
                pltpu.make_async_copy(whole.at[3 * layer + 1, :, :, n // 2, n % 2], ubuf.at[slot], load_sem.at[slot, 0]),
                pltpu.make_async_copy(slope_in.at[layer, n], slopebuf.at[slot], load_sem.at[slot, 2]),
            ],
            load_down(whole, 3 * layer + 2, n, dbuf.at[slot], load_sem.at[slot, 3]),
        )

    def act_copy(layer, n, slot):
        return pltpu.make_async_copy(act_in.at[layer, n], actbuf.at[slot], load_sem.at[slot, 1])

    def start_all(layer, n, slot):
        some, more = copies(layer, n, slot)
        for copy in some + more:
            copy.start()

    def wait_all(layer, n, slot):
        for copy in copies(layer, n, slot)[0]:
            copy.wait()
        wait_for(dbuf.at[slot], load_sem.at[slot, 3])

    def norm_back(layer, grad, unit, scale, row):
        vec[row[0] : row[0] + 1, :] = jnp.sum(grad * unit, axis=0, keepdims=True)
        vec[row[1] : row[1] + 1, :] = jnp.sum(grad, axis=0, keepdims=True)
        scaled = grad * gain[layer, row[2] : row[2] + 1, :]
        return (
            scaled
            - jnp.mean(scaled, axis=-1, keepdims=True)
            - unit * jnp.mean(scaled * unit, axis=-1, keepdims=True)
        ) * scale

    ways = [place.at(c=1 - place.c), place.at(y=1 - place.y), place.at(b=1 - place.b)]
    line = vec_line.at[pl.ds(0, LINES - 1)]

    def send_vec(k):
        if k < 3:
            push(vec, vec_got.at[k], vec_send.at[k], vec_recv.at[k], ways[k])
            return
        for o in range(1, LINES):
            push(vec, vec_line.at[place.a], vec_send.at[3], vec_recv.at[3], place.at(a=(place.a + o) % LINES))

    def add_vec(k):
        if k < 3:
            wait_for(vec, vec_send.at[k])
            wait_for(vec_got.at[k], vec_recv.at[k])
            vec[...] += vec_got[k]
            return
        wait_for(line, vec_send.at[3])
        wait_for(line, vec_recv.at[3])
        vec_line[place.a] = vec[...]
        vec[...] = (vec_line[0] + vec_line[1]) + (vec_line[2] + vec_line[3])

    for layer in reversed(range(LAYERS)):
        base = 12 * layer
        early = [
            pltpu.make_async_copy(n2_in.at[layer], unit, misc_sem.at[0]),
            pltpu.make_async_copy(nl_in.at[layer], nl, misc_sem.at[1]),
            pltpu.make_async_copy(ctx_in.at[layer], ctx, misc_sem.at[2]),
            pltpu.make_async_copy(qkv_in.at[layer], qkv, misc_sem.at[3]),
        ]
        act_copy(layer, 0, 0).start()
        for copy in early:
            copy.start()
        start_all(layer, 0, 0)
        for copy in early[:2]:
            copy.wait()
        second[...] = norm_back(
            layer, stream[...], unit[...], scale_in[:, 2 * layer + 1 : 2 * layer + 2], (base + 9, base + 11, 1)
        )
        go[...] = second[...].astype(BF)
        go_t[...] = go[...].T
        nl_t[...] = nl[...].T
        late = [
            pltpu.make_async_copy(n1_in.at[layer], unit, misc_sem.at[0]),
            pltpu.make_async_copy(hid2 if layer == 1 else x, nl, misc_sem.at[1]),
        ]
        for copy in late:
            copy.start()
        vec[base + 3 : base + 4, :] = jnp.sum(go[...].astype(F32), axis=0, keepdims=True)
        acc[...] = second[...]
        if layer == 1:
            place.meet()
        clock.until(0 if layer == 1 else PARTS + 1)

        def down_grad(n):
            slot = n % 2
            act_copy(layer, n, slot).wait()

            @pl.when(n < 3)
            def _():
                act_copy(layer, n + 1, 1 - slot).start()

            for b in range(2):
                down = nn(go_t[...], actbuf[slot, :, b * 384 : b * 384 + 384]).astype(BF)
                for m in range(4):
                    for h in range(2):
                        grads[2, n, b, m // 2, m % 2, :, h * 384 : h * 384 + 384] = down[
                            192 * m + BLOCK * h : 192 * m + BLOCK * h + BLOCK, :
                        ]

        clock.loop(4, down_grad, 0 if layer == 1 else 1)
        clock.until(1 if layer == 1 else 2 * PARTS + 1)

        def chunk(n):
            slot = n % 2
            wait_all(layer, n, slot)

            @pl.when(n < 3)
            def _():
                start_all(layer, n + 1, 1 - slot)

            outer = go[...]
            wide = jnp.concatenate([nn(outer, dbuf[slot, 0]), nn(outer, dbuf[slot, 1])], axis=1)
            pre = (wide * slopebuf[slot].astype(F32)).astype(BF)
            vec[pl.ds(base + 4 + n, 1), :] = jnp.sum(pre.astype(F32), axis=0, keepdims=True)
            acc[...] += nt(pre, panel(ubuf[slot]))
            up = nn(nl_t[...], pre).astype(BF)
            grads[1, :, :, n // 2, n % 2] = up.reshape(LINES, 2, BLOCK, WIDE)

        clock.loop(4, chunk, 2 if layer == 1 else 4)

        def side_copy(n):
            return pltpu.make_async_copy(whole.at[3 * layer, :, :, n // 2, n % 2], ubuf.at[n % 2], load_sem.at[n % 2, 0])

        side_copy(0).start()
        side_copy(1).start()
        for copy in late + early[2:]:
            copy.wait()
        second[...] = norm_back(layer, acc[...], unit[...], scale_in[:, 2 * layer : 2 * layer + 1], (base + 8, base + 10, 0))
        go[...] = second[...].astype(BF)
        vec[base + 2 : base + 3, :] = jnp.sum(go[...].astype(F32), axis=0, keepdims=True)

        def tile_of(index):
            return go[:, index * 128 : index * 128 + 128]

        zero = jnp.zeros((), BF)
        outs = []
        for pair in range(2):
            mixed = turn(tile_of(3 * pair + 1).astype(F32)).astype(BF)
            outs.append((jnp.where(low, zero, mixed), tile_of(3 * pair)))
            outs.append((jnp.where(low, mixed, zero), tile_of(3 * pair + 2)))
        acc[...] = jnp.zeros_like(acc)
        for n in range(4):
            near = slice(512, 640) if n % 2 == 0 else slice(0, 128)
            side_copy(n).wait()
            acc[...] += nt(outs[n][0], panel(ubuf[n % 2, :, :, :, near])) + nt(
                outs[n][1], panel(ubuf[n % 2, :, :, :, 640:768])
            )
            side_copy((n + 2) % 4).start()
        for pair in range(6):
            gctx[pair] = acc[:, pair * 128 : pair * 128 + 128].astype(BF)

        if layer == 1:
            clock.until(PARTS + 1)
        above = logit_grad if layer == LAYERS - 1 else carry

        def fetch(pair, slot):
            return [
                pltpu.make_async_copy(soft_in.at[layer, pl.ds(pair * 2, 2)], soft.at[slot], soft_sem.at[0, slot]),
                pltpu.make_async_copy(above.at[pl.ds(pair * 2, 2)], dc_in.at[slot], soft_sem.at[1, slot]),
            ]

        for copy in fetch(0, 0):
            copy.start()

        def two_heads(pair):
            slot = pair % 2
            for copy in fetch(pair, slot):
                copy.wait()

            @pl.when(pair < 5)
            def _():
                for copy in fetch(pair + 1, 1 - slot):
                    copy.start()

            if layer > 0:

                @pl.when(pair >= 2)
                def _():
                    pltpu.make_async_copy(dc_out.at[slot], carry.at[pl.ds(0, 2)], soft_sem.at[2, slot]).wait()

            queries, keys, values, grad = qkv[pair], qkv[6 + pair], qkv[12 + pair], gctx[pair]
            both = grad.astype(F32) * ctx[pair].astype(F32)
            grad_q, grad_k, grad_v = 0.0, 0.0, 0.0
            for head in range(2):
                mine = low if head == 0 else ~low
                own = jnp.where(mine, grad, zero)
                dot = jnp.sum(jnp.where(mine, both, 0.0), axis=-1, keepdims=True)
                share = soft[slot, head]
                inner = nt(own, values)
                scores = (share.astype(F32) * (inner - dot) + dc_in[slot, head].astype(F32)).astype(BF)
                dc_out[slot, head] = scores
                grad_v = grad_v + tn(share, own)
                grad_q = grad_q + nn(scores, jnp.where(mine, keys, zero))
                grad_k = grad_k + tn(scores, jnp.where(mine, queries, zero))
            gqkv[pair] = (grad_q * HEAD_DIM**-0.5).astype(BF)
            gqkv[6 + pair] = grad_k.astype(BF)
            gqkv[12 + pair] = grad_v.astype(BF)
            if layer > 0:
                pltpu.make_async_copy(dc_out.at[slot], carry.at[pl.ds(pair * 2, 2)], soft_sem.at[2, slot]).start()

        clock.loop(6, two_heads, 2 if layer == 1 else 3)
        if layer > 0:
            for slot in range(2):
                pltpu.make_async_copy(dc_out.at[slot], carry.at[pl.ds(0, 2)], soft_sem.at[2, slot]).wait()
        for group in range(6):
            lanes = slice(group * 128, group * 128 + 128)
            vec[base : base + 1, lanes] = jnp.sum(gqkv[group].astype(F32), axis=0, keepdims=True)
            vec[base + 1 : base + 2, lanes] = jnp.sum(gqkv[12 + group].astype(F32), axis=0, keepdims=True)

        if layer == 0:
            send_vec(0)

        nl_t[...] = nl[...].T
        go_t[...] = jnp.concatenate([ctx[pair] for pair in range(6)], axis=1).T
        clock.until(2 * PARTS if layer == 1 else 3 * PARTS + 1)
        stream[...] = second[...]
        for n in range(4):
            pair = n // 2
            if n % 2 == 0:
                tiles = [gqkv[9 * pair + k] for k in range(4)] + [jnp.where(low, gqkv[9 * pair + 4], zero)]
            else:
                tiles = [jnp.where(low, zero, gqkv[9 * pair + 4])] + [gqkv[9 * pair + k] for k in range(5, 9)]
            side = jnp.concatenate(tiles, axis=1)
            side_copy(n).wait()
            stream[...] += nt(side, panel(ubuf[n % 2, :, :, :, 0:640]))
            if n < 2:
                side_copy(n + 2).start()
            first = nn(nl_t[...], side)
            near = nn(go_t[...], outs[n][0])
            far = nn(go_t[...], outs[n][1])
            shape = (LINES, 2, BLOCK, 128)
            mixed = 4 if n % 2 == 0 else 0
            for tile in range(5):
                value = first[:, tile * 128 : tile * 128 + 128]
                if tile == mixed:
                    value = value + near
                grads[0, :, :, n // 2, n % 2, :, tile * 128 : tile * 128 + 128] = value.astype(BF).reshape(shape)
            grads[0, :, :, n // 2, n % 2, :, 640:768] = far.astype(BF).reshape(shape)
            if layer == 0:
                if n % 2 == 1:
                    add_vec(n // 2)
                    send_vec(n // 2 + 1)
    grad_in[...] = stream[...].astype(BF)
    clock.until(ROUNDS - 2)
    add_vec(2)
    send_vec(3)
    clock.until(ROUNDS)
    add_vec(3)
    clock.until(ROUNDS + GAP + 4)


def forward(runs, mats, x, segments, bias, up_bias, gain, shift):
    length, width = x.shape
    heads = width // HEAD_DIM
    sds = jax.ShapeDtypeStruct
    vmem, hbm = pl.BlockSpec(memory_space=pltpu.VMEM), pl.BlockSpec(memory_space=pltpu.HBM)
    outs = [
        (sds((length, width), BF), vmem),
        (sds((heads, length, length), BF), hbm),
        (sds((LAYERS, heads, length, length), BF), hbm),
        (sds((LAYERS, 18, length, 128), BF), hbm),
        (sds((LAYERS, 6, length, 128), BF), hbm),
        (sds((length, width), BF), hbm),
        (sds((LAYERS, length, width), BF), hbm),
        (sds((LAYERS, 4, length, width), BF), hbm),
        (sds((LAYERS, 4, length, width), BF), hbm),
        (sds((LAYERS, length, width), F32), hbm),
        (sds((LAYERS, length, width), F32), hbm),
        (sds((length, 2 * LAYERS), F32), vmem),
    ]
    outs.append((sds((6, LINES, 2, 2, 2, BLOCK, WIDE), BF), hbm))
    dma = pltpu.SemaphoreType.DMA
    scratch = [
        pltpu.VMEM((length, width), F32),
        pltpu.VMEM((LAYERS, 18, length, 128), BF),
        pltpu.VMEM((6, length, 128), BF),
        pltpu.VMEM((length, width), F32),
        pltpu.VMEM((length, width), F32),
        pltpu.VMEM((length, width), F32),
        pltpu.VMEM((length, width), BF),
        pltpu.VMEM((length, width), BF),
        pltpu.VMEM((4, length, width), BF),
        pltpu.VMEM((4, length, width), BF),
        pltpu.VMEM((length, length), F32),
        pltpu.VMEM((2, 2, length, length), BF),
        pltpu.VMEM((2, 2, length, length), BF),
        pltpu.VMEM((4, LINES, 2, BLOCK, WIDE), BF),
        pltpu.VMEM((4, LINES, 2, BLOCK, WIDE), BF),
        pltpu.VMEM((LINES, 2, WIDE, 384), BF),
        dma((4,)),
        dma((2, 2)),
        dma((9,)),
        dma(()),
        dma((ROUNDS, 2, 4)),
        dma((ROUNDS, 2, 7)),
        pltpu.VMEM((6, BLOCK, WIDE), BF),
        pltpu.VMEM((BLOCK, 640), F32),
        pltpu.VMEM((BLOCK, 256), F32),
    ]
    return pl.pallas_call(
        functools.partial(forward_kernel, runs),
        out_shape=[o[0] for o in outs],
        in_specs=[vmem] * 10,
        out_specs=[o[1] for o in outs],
        scratch_shapes=scratch,
        compiler_params=pltpu.CompilerParams(vmem_limit_bytes=60 << 20, collective_id=0, has_side_effects=True),
        name="ahead",
    )(*mats, x, segments, bias, up_bias, gain, shift)


def backward(runs, whole, x, kept, out_grad, logit_grad, gain):
    soft, qkv, ctx, hid2, nl, act, slope, n1, n2, scale = kept
    length, width = x.shape
    heads = width // HEAD_DIM
    sds = jax.ShapeDtypeStruct
    vmem, hbm = pl.BlockSpec(memory_space=pltpu.VMEM), pl.BlockSpec(memory_space=pltpu.HBM)
    blocks = (LINES, 2, 2, 2, BLOCK, WIDE)
    outs = [
        (sds((length, width), BF), vmem),
        (sds((6, BLOCK, WIDE), F32), vmem),
        (sds((12 * LAYERS, width), F32), vmem),
        (sds((heads, length, length), BF), hbm),
    ]
    dma = pltpu.SemaphoreType.DMA
    scratch = [
        pltpu.VMEM((length, width), F32),
        pltpu.VMEM((length, width), F32),
        pltpu.VMEM((length, width), F32),
        pltpu.VMEM((length, width), BF),
        pltpu.VMEM((width, length), BF),
        pltpu.VMEM((length, width), BF),
        pltpu.VMEM((width, length), BF),
        pltpu.VMEM((length, width), F32),
        pltpu.VMEM((6, length, 128), BF),
        pltpu.VMEM((6, length, 128), BF),
        pltpu.VMEM((18, length, 128), BF),
        pltpu.VMEM((18, length, 128), BF),
        pltpu.VMEM((2, LINES, 2, BLOCK, WIDE), BF),
        pltpu.VMEM((2, 2, WIDE, 384), BF),
        pltpu.VMEM((2, length, width), BF),
        pltpu.VMEM((2, length, width), BF),
        pltpu.VMEM((2, 2, length, length), BF),
        pltpu.VMEM((2, 2, length, length), BF),
        pltpu.VMEM((2, 2, length, length), BF),
        dma((2, 4)),
        dma((4,)),
        dma((3, 2)),
        pltpu.VMEM((3,) + blocks, BF),
        pltpu.VMEM((SETS, 2, 2, LINES, 2, PIECE, WIDE), BF),
        pltpu.VMEM((SETS, LINES, 2, PIECE, WIDE), BF),
        pltpu.VMEM((SETS, 2, LINES, PIECE, WIDE), BF),
        pltpu.VMEM((SETS, 2, LINES, PIECE, WIDE), BF),
        pltpu.VMEM((SETS, 2, LINES - 1, PIECE, WIDE), BF),
        dma((SETS, 2, 4)),
        dma((SETS, 2, 4)),
        pltpu.SemaphoreType.REGULAR((SETS,)),
        pltpu.VMEM((3, 12 * LAYERS, width), F32),
        pltpu.VMEM((LINES, 12 * LAYERS, width), F32),
        dma((4,)),
        dma((4,)),
    ]
    return pl.pallas_call(
        functools.partial(backward_kernel, runs),
        out_shape=[o[0] for o in outs],
        in_specs=[hbm] * 10 + [vmem, hbm, vmem, hbm, vmem],
        out_specs=[o[1] for o in outs],
        scratch_shapes=scratch,
        compiler_params=pltpu.CompilerParams(vmem_limit_bytes=62 << 20, collective_id=1, has_side_effects=True),
        name="back",
    )(whole, x, hid2, qkv, ctx, nl, act, slope, n1, n2, scale, soft, out_grad, logit_grad, gain)


def finish_kernel(owned, vec, result_in, grad_in, logits_in, result, logits, grad, g_qkv, g_out, g_up, g_down,
                  g_bias, g_up_bias, g_gain, g_shift, stage, sem):
    heads = logits.shape[0]
    count = stage.shape[0]
    step = heads // count
    parts = [pl.ds(k * step, step) for k in range(count)]
    for k, at in enumerate(parts):
        pltpu.make_async_copy(logits_in.at[at], stage.at[k], sem.at[0, k]).start()
    result[...] = result_in[...]
    grad[...] = grad_in[...]
    odd = lax.broadcasted_iota(jnp.int32, (1, 128), 1) * 0 + lax.axis_index("narrow") % 2 == 1
    low = low_lanes((1, 128))
    for layer in range(LAYERS):
        block = owned[3 * layer]
        moved = pltpu.roll(block, WIDE - HEAD_DIM, 1)
        for k in range(5):
            lanes = slice(k * 128, min(k * 128 + 128, 576))
            tile = slice(k * 128, k * 128 + 128)
            g_qkv[layer, :, lanes] = jnp.where(odd, moved[:, tile], block[:, tile])[:, : lanes.stop - lanes.start]
        last = block[:, 640:768]
        g_out[layer, :, 0:128] = jnp.where(odd, jnp.where(low, block[:, 0:128], turn(last)), last)
        g_out[layer, :, 128:192] = jnp.where(odd, turn(last), turn(block[:, 512:640]))[:, 0:64]
        g_up[layer] = owned[3 * layer + 1]
        down = owned[3 * layer + 2]
        g_down[layer, 0:BLOCK, :] = down[:, 0:384]
        g_down[layer, BLOCK : 2 * BLOCK, :] = down[:, 384:768]
        base = 12 * layer
        g_bias[layer] = vec[base : base + 4, :]
        for n in range(4):
            g_up_bias[layer : layer + 1, n * WIDE : n * WIDE + WIDE] = vec[base + 4 + n : base + 5 + n, :]
        g_gain[layer] = vec[base + 8 : base + 10, :]
        g_shift[layer] = vec[base + 10 : base + 12, :]
    for k, at in enumerate(parts):
        pltpu.make_async_copy(logits_in.at[at], stage.at[k], sem.at[0, k]).wait()
        pltpu.make_async_copy(stage.at[k], logits.at[at], sem.at[1, k]).start()
    for k, at in enumerate(parts):
        pltpu.make_async_copy(stage.at[k], logits.at[at], sem.at[1, k]).wait()


def finish(owned, vec, result, grad, logits):
    sds = jax.ShapeDtypeStruct
    vmem, hbm = pl.BlockSpec(memory_space=pltpu.VMEM), pl.BlockSpec(memory_space=pltpu.HBM)
    heads, length, _ = logits.shape
    outs = [
        (sds(result.shape, BF), vmem),
        (sds(logits.shape, BF), hbm),
        (sds(grad.shape, BF), vmem),
        (sds((LAYERS, BLOCK, 576), F32), vmem),
        (sds((LAYERS, BLOCK, 192), F32), vmem),
        (sds((LAYERS, BLOCK, WIDE), F32), vmem),
        (sds((LAYERS, 2 * BLOCK, 384), F32), vmem),
        (sds((LAYERS, 4, WIDE), F32), vmem),
        (sds((LAYERS, 4 * WIDE), F32), vmem),
        (sds((LAYERS, 2, WIDE), F32), vmem),
        (sds((LAYERS, 2, WIDE), F32), vmem),
    ]
    return pl.pallas_call(
        finish_kernel,
        out_shape=[o[0] for o in outs],
        in_specs=[vmem] * 4 + [hbm],
        out_specs=[o[1] for o in outs],
        scratch_shapes=[pltpu.VMEM((6, heads // 6, length, length), BF), pltpu.SemaphoreType.DMA((2, 6))],
        compiler_params=pltpu.CompilerParams(vmem_limit_bytes=48 << 20),
        name="finish",
    )(owned, vec, result, grad, logits)


def body(runs, inputs, segments, out_grad, logit_grad, w_qkv, w_out, w_up, w_down, biases, up_bias, gains, shifts):
    mats = [w_qkv, w_out, w_up, w_down]
    groups = [[g * runs + r for r in range(runs)] for g in range(2 * LINES)]
    if runs > 1:
        mats = [lax.all_gather(w.astype(BF), "dp", axis_index_groups=groups, axis=1, tiled=True) for w in mats]
    result, logits, *kept, whole = forward(runs, mats[:3] + [jnp.swapaxes(mats[3], 1, 2)], inputs[0], segments, biases, up_bias, gains, shifts)
    grad_in, owned, vec, _ = backward(runs, whole, inputs[0], kept, out_grad[0], logit_grad[0], gains)
    result, logits, grad_in, *grads = finish(owned, vec, result, grad_in, logits)
    grads[3] = jnp.swapaxes(grads[3], 1, 2)
    if runs > 1:
        grads = [
            lax.psum_scatter(g, "dp", axis_index_groups=groups, scatter_dimension=1, tiled=True) for g in grads[:4]
        ] + list(lax.psum(tuple(grads[4:]), "dp", axis_index_groups=groups))
    return (result[None], logits[None], grad_in[None], *grads)


def solution(mesh):
    rows = P(("dp", "narrow"), None, None)
    heads = P(("dp", "narrow"), None, None, None)
    blocks = P(None, "dp", "narrow")
    runs = mesh.shape["dp"] // (2 * LINES)
    return jax.shard_map(
        functools.partial(body, runs),
        mesh=mesh,
        in_specs=(rows, P(("dp", "narrow"), None), rows, heads) + (blocks,) * 4 + (P(),) * 4,
        out_specs=(rows, heads, rows) + (blocks,) * 4 + (P(),) * 4,
        check_vma=False,
    )
```

```python
import functools

import jax
import jax.numpy as jnp
from jax import lax
import jax.experimental.pallas as pl
import jax.experimental.pallas.tpu as pltpu
from jax.sharding import PartitionSpec as P

BF, F32 = jnp.bfloat16, jnp.float32
MESH = pl.DeviceIdType.MESH
HEAD_DIM = 64
LAYERS = 2
EPS = 1e-6
MASKED = -1e30

LINES = 4
BLOCK = 96
HALF = BLOCK // 2
WIDE = 768
PARTS = 3
PIECE = HALF // PARTS
ROUNDS = 6 * PARTS
AHEAD = 4
GAP = 0
SETS = 7


def nn(left, right):
    return lax.dot_general(left, right, (((1,), (0,)), ((), ())), preferred_element_type=F32)


def nt(left, right):
    return lax.dot_general(left, right, (((1,), (1,)), ((), ())), preferred_element_type=F32)


def tn(left, right):
    return lax.dot_general(left, right, (((0,), (0,)), ((), ())), preferred_element_type=F32)


def low_lanes(shape):
    return lax.broadcasted_iota(jnp.int32, shape, len(shape) - 1) % 128 < HEAD_DIM


def turn(tile):
    return pltpu.roll(tile, HEAD_DIM, 1)


class Place:
    def __init__(self, runs):
        d, n = lax.axis_index("dp"), lax.axis_index("narrow")
        self.runs, self.run = runs, d % runs
        self.a, self.b, self.y, self.c = d // runs // 2, d // runs % 2, n // 2, n % 2

    def at(self, a=None, b=None, y=None, c=None):
        a = self.a if a is None else a
        b = self.b if b is None else b
        y = self.y if y is None else y
        c = self.c if c is None else c
        return ((a * 2 + b) * self.runs + self.run, y * 2 + c)

    def peers(self):
        lines = [self.at(a=(self.a + o) % LINES) for o in range(1, LINES)]
        return lines + [self.at(b=1 - self.b), self.at(y=1 - self.y), self.at(c=1 - self.c)]

    def greet(self):
        for peer in self.peers():
            pl.semaphore_signal(pltpu.get_barrier_semaphore(), inc=1, device_id=peer, device_id_type=MESH)

    def meet(self):
        pl.semaphore_wait(pltpu.get_barrier_semaphore(), len(self.peers()))


def push(src, dst, send, recv, to):
    pltpu.make_async_remote_copy(
        src_ref=src, dst_ref=dst, send_sem=send, recv_sem=recv, device_id=to, device_id_type=MESH
    ).start()


def wait_for(view, sem):
    pltpu.make_async_copy(view, view, sem).wait()


class Gather:
    def __init__(self, place, whole, send, recv):
        self.p, self.whole, self.send, self.recv = place, whole, send, recv

    def rows(self, t, half):
        return pl.ds(pl.multiple_of(half * HALF + (t % PARTS) * PIECE, 16), PIECE)

    def line(self, t, half, b, y, c):
        return self.whole.at[t // PARTS, :, b, y, c, self.rows(t, half), :]

    def stage1(self, t):
        p = self.p
        for half in range(2):
            mine = self.whole.at[t // PARTS, p.a, p.b, p.y, p.c, self.rows(t, half), :]
            for o in range(1, LINES):
                push(mine, mine, self.send.at[t, half, 0], self.recv.at[t, half, 0], p.at(a=(p.a + o) % LINES))

    def first(self, half):
        p = self.p
        return (1 - p.b, p.y) if half == 0 else (p.b, 1 - p.y)

    def second(self, half):
        p = self.p
        return (p.b, 1 - p.y) if half == 0 else (1 - p.b, p.y)

    def stage2(self, t):
        p = self.p
        for half in range(2):
            some = self.whole.at[t // PARTS, pl.ds(0, LINES - 1), 0, 0, 0, self.rows(t, half), :]
            wait_for(some, self.recv.at[t, half, 0])
            line = self.line(t, half, p.b, p.y, p.c)
            b1, y1 = self.first(half)
            b2, y2 = self.second(half)
            push(line, line, self.send.at[t, half, 1], self.recv.at[t, half, 1], p.at(b=b1, y=y1))
            push(line, line, self.send.at[t, half, 2], self.recv.at[t, half, 2], p.at(b=b2, y=y2))
            push(line, line, self.send.at[t, half, 3], self.recv.at[t, half, 4], p.at(c=1 - p.c))

    def stage3(self, t):
        p = self.p
        for half in range(2):
            b1, y1 = self.first(half)
            b2, y2 = self.second(half)
            line = self.line(t, half, b1, y1, p.c)
            wait_for(line, self.recv.at[t, half, 1])
            push(line, line, self.send.at[t, half, 2], self.recv.at[t, half, 3], p.at(b=b2, y=y2))
            push(line, line, self.send.at[t, half, 3], self.recv.at[t, half, 5], p.at(c=1 - p.c))

    def stage4(self, t):
        p = self.p
        for half in range(2):
            b2, y2 = self.second(half)
            far = self.line(t, half, b2, y2, p.c)
            wait_for(far, self.recv.at[t, half, 2])
            push(far, far, self.send.at[t, half, 3], self.recv.at[t, half, 6], p.at(c=1 - p.c))
            far = self.line(t, half, 1 - p.b, 1 - p.y, p.c)
            wait_for(far, self.recv.at[t, half, 3])
            push(far, far, self.send.at[t, half, 3], self.recv.at[t, half, 6], p.at(c=1 - p.c))

    def stage5(self, t):
        for half in range(2):
            line = self.line(t, half, 0, 0, 0)
            wait_for(line, self.recv.at[t, half, 4])
            wait_for(line, self.recv.at[t, half, 5])
            two = self.whole.at[t // PARTS, :, :, 0, 0, self.rows(t, half), :]
            wait_for(two, self.recv.at[t, half, 6])
            some = self.whole.at[t // PARTS, pl.ds(0, LINES - 1), 0, 0, 0, self.rows(t, half), :]
            wait_for(some, self.send.at[t, half, 0])
            wait_for(line, self.send.at[t, half, 1])
            wait_for(two, self.send.at[t, half, 2])
            four = self.whole.at[t // PARTS, :, :, :, 0, self.rows(t, half), :]
            wait_for(four, self.send.at[t, half, 3])

    def round(self, t):
        @pl.when(t < ROUNDS)
        def _():
            self.stage2(t)

        @pl.when(t + AHEAD < ROUNDS)
        def _():
            self.stage1(t + AHEAD)

        @pl.when((t >= 1) & (t - 1 < ROUNDS))
        def _():
            self.stage3(t - 1)

        @pl.when((t >= 2 + PARTS) & (t - 2 < ROUNDS))
        def _():
            self.stage4(t - 2)

        @pl.when((t >= 3 + PARTS) & (t - 3 < ROUNDS))
        def _():
            self.stage5(t - 3)

    def begin(self):
        def loop(start, stop, stage):
            def step(t, _):
                stage(t)
                return 0

            lax.fori_loop(start, stop, step, 0)

        loop(0, PARTS, self.stage1)
        loop(0, PARTS, self.stage2)
        loop(PARTS, PARTS + 1 + AHEAD, self.stage1)
        loop(0, PARTS, self.stage3)
        self.stage2(PARTS)
        loop(0, PARTS, self.stage4)
        loop(0, PARTS, self.stage5)
        return PARTS + 1


class Reduce:
    def __init__(self, place, grads, owned, got1, got2a, got2b, got3, got4, send, recv, free):
        self.p, self.grads, self.owned = place, grads, owned
        self.got1, self.got2, self.got3, self.got4 = got1, (got2a, got2b), got3, got4
        self.send, self.recv, self.free = send, recv, free

    def rows(self, t, half):
        return pl.ds(pl.multiple_of(half * HALF + (t % PARTS) * PIECE, 16), PIECE)

    def mat(self, t):
        return 2 - (t // PARTS) % 3

    def stage1(self, t):
        p, s = self.p, t % SETS

        @pl.when(t >= SETS)
        def _():
            pl.semaphore_wait(self.free.at[s], LINES + 2)

        for half in range(2):
            for y in range(2):
                push(
                    self.grads.at[self.mat(t), :, :, y, 1 - p.c, self.rows(t, half), :],
                    self.got1.at[s, half, y],
                    self.send.at[s, half, 0],
                    self.recv.at[s, half, 0],
                    p.at(c=1 - p.c),
                )

    def stage2(self, t):
        p, s = self.p, t % SETS
        for half in range(2):
            wait_for(self.got1.at[s, half], self.recv.at[s, half, 0])
            rows = self.rows(t, half)
            for y in range(2):
                self.got1[s, half, y] = self.got1[s, half, y] + self.grads[self.mat(t), :, :, y, p.c, rows, :]
            if half == 0:
                push(
                    self.got1.at[s, half, 1 - p.y],
                    self.got2[0].at[s],
                    self.send.at[s, half, 1],
                    self.recv.at[s, half, 1],
                    p.at(y=1 - p.y),
                )
            else:
                push(
                    self.got1.at[s, half, :, :, 1 - p.b],
                    self.got2[1].at[s],
                    self.send.at[s, half, 1],
                    self.recv.at[s, half, 1],
                    p.at(b=1 - p.b),
                )
        for half in range(2):
            wait_for(self.got1.at[s, half], self.send.at[s, half, 0])

    def stage3(self, t):
        p, s = self.p, t % SETS
        for half in range(2):
            got = self.got2[half]
            wait_for(got.at[s], self.recv.at[s, half, 1])
            if half == 0:
                got[s] = got[s] + self.got1[s, half, p.y]
                src, to = got.at[s, :, 1 - p.b], p.at(b=1 - p.b)
            else:
                got[s] = got[s] + self.got1[s, half, :, :, p.b]
                src, to = got.at[s, 1 - p.y], p.at(y=1 - p.y)
            push(src, self.got3.at[s, half], self.send.at[s, half, 2], self.recv.at[s, half, 2], to)

    def stage4(self, t):
        p, s = self.p, t % SETS
        for half in range(2):
            wait_for(self.got3.at[s, half], self.recv.at[s, half, 2])
            mine = self.got2[0][s, :, p.b] if half == 0 else self.got2[1][s, p.y]
            self.got3[s, half] = self.got3[s, half] + mine
            for o in range(1, LINES):
                a = (p.a + o) % LINES
                push(
                    self.got3.at[s, half, a],
                    self.got4.at[s, half, o - 1],
                    self.send.at[s, half, 3],
                    self.recv.at[s, half, 3],
                    p.at(a=a),
                )

    def stage5(self, t):
        p, s = self.p, t % SETS
        for half in range(2):
            wait_for(self.got4.at[s, half], self.recv.at[s, half, 3])
            total = self.got3[s, half, p.a].astype(F32)
            for o in range(LINES - 1):
                total = total + self.got4[s, half, o].astype(F32)
            self.owned[5 - t // PARTS, self.rows(t, half), :] = total
            wait_for(self.got2[half].at[s], self.send.at[s, half, 1])
            wait_for(self.got3.at[s, half], self.send.at[s, half, 2])
            wait_for(self.got4.at[s, half], self.send.at[s, half, 3])

        @pl.when(t + SETS < ROUNDS)
        def _():
            for peer in p.peers():
                pl.semaphore_signal(self.free.at[s], inc=1, device_id=peer, device_id_type=MESH)

    def round(self, v):
        last = ROUNDS - PARTS
        for lag, stage in enumerate((self.stage1, self.stage2, self.stage3, self.stage4, self.stage5)):
            t = v - lag

            @pl.when((t >= 0) & (t < last))
            def _(stage=stage, t=t):
                stage(t)

            @pl.when((t >= last + GAP) & (t < ROUNDS + GAP))
            def _(stage=stage, t=t):
                stage(t - GAP)


class Clock:
    def __init__(self, transfer):
        self.transfer, self.done = transfer, 0

    def until(self, count):
        if count > self.done:

            def step(t, _):
                self.transfer.round(t)
                return 0

            lax.fori_loop(self.done, count, step, 0)
            self.done = count

    def loop(self, count, work, rounds):
        start = self.done

        def step(i, _):
            work(i)
            if rounds > 0:

                @pl.when(((i + 1) * rounds) // count > (i * rounds) // count)
                def _():
                    self.transfer.round(start + (i * rounds) // count)

            return 0

        lax.fori_loop(0, count, step, 0)
        self.done = start + rounds


def gelu_and_slope(values):
    size = jnp.abs(values)
    below = 1.0 + (0.3275911 * 0.7071067811865476) * size
    rough = pl.reciprocal(below, approx=True)
    t = rough * (2.0 - below * rough)
    bell = jnp.exp(-0.5 * values * values)
    poly = t * (
        0.5 * 0.254829592
        + t * (0.5 * -0.284496736 + t * (0.5 * 1.421413741 + t * (0.5 * -1.453152027 + t * (0.5 * 1.061405429))))
    )
    tail = poly * bell
    phi = jnp.where(values < 0, tail, 1.0 - tail)
    return values * phi, phi + values * (bell * 0.3989422804014327)


def standardize(values):
    centred = values - jnp.mean(values, axis=-1, keepdims=True)
    scale = lax.rsqrt(jnp.mean(centred * centred, axis=-1, keepdims=True) + EPS)
    return centred * scale, scale


def load_mat(whole, index, buffer, sem):
    return [
        pltpu.make_async_copy(whole.at[index, :, :, n // 2, n % 2], buffer.at[n], sem.at[n]) for n in range(4)
    ]


def load_down(whole, index, a, buffer, sem):
    out = []
    for n in range(4):
        for h in range(2):
            src = whole.at[index, a, :, n // 2, n % 2, :, pl.ds(h * 384, 384)]
            out.append(pltpu.make_async_copy(src, buffer.at[:, pl.ds(192 * n + BLOCK * h, BLOCK), :], sem))
    return out


def panel(block):
    return block.reshape(WIDE, block.shape[-1])


def forward_kernel(
    runs, w_qkv, w_out, w_up, w_down, x, segments, bias, up_bias, gain, shift,
    result, logits, soft_out, qkv_out, ctx_out, hid_out, nl_out, act_out, slope_out, n1_out, n2_out, scale_out, *rest
):
    (whole, stream, qkv, ctx, normed, n1, n2, nl, hid, act, slope, penalty, soft, logit, mat_c, mat_u, mat_d,
     load_sem, soft_sem, save_sem, own_sem, send, recv, own, pad_qkv, pad_out) = rest
    place = Place(runs)
    place.greet()
    odd = lax.broadcasted_iota(jnp.int32, (1, 128), 1) * 0 + place.c == 1
    low = low_lanes((1, 128))
    for layer in range(LAYERS):
        pad_qkv[:, 0:576] = w_qkv[layer].astype(F32)
        pad_out[:, 0:192] = w_out[layer].astype(F32)
        plain = pad_qkv[...]
        moved = pltpu.roll(plain, HEAD_DIM, 1)
        near, far = pad_out[:, 0:128], pad_out[:, 128:256]
        tiles = [(plain[:, k * 128 : k * 128 + 128], moved[:, k * 128 : k * 128 + 128]) for k in range(5)]
        tiles[4] = (jnp.where(low, tiles[4][0], turn(far)), tiles[4][1])
        tiles[0] = (tiles[0][0], jnp.where(low, near, tiles[0][1]))
        tiles.append((near, jnp.where(low, turn(near), turn(far))))
        for k, (even_form, odd_form) in enumerate(tiles):
            own[3 * layer, :, k * 128 : k * 128 + 128] = jnp.where(odd, odd_form, even_form).astype(BF)
        own[3 * layer + 1] = w_up[layer].astype(BF)
        own[3 * layer + 2, :, 0:384] = w_down[layer, 0:BLOCK, :].astype(BF)
        own[3 * layer + 2, :, 384:768] = w_down[layer, BLOCK : 2 * BLOCK, :].astype(BF)
    own_copy = pltpu.make_async_copy(own, whole.at[:, place.a, place.b, place.y, place.c], own_sem)
    own_copy.start()
    gather = Gather(place, whole, send, recv)
    row = segments[...].astype(F32)
    column = jnp.broadcast_to(row, (8, row.shape[1])).T[:, 0:1]
    penalty[...] = jnp.where(column == row, 0.0, MASKED)
    stream[...] = x[...].astype(F32)
    own_copy.wait()
    place.meet()
    clock = Clock(gather)
    clock.done = gather.begin()

    def arrived(index):
        if index > 0:
            clock.until(PARTS * index + PARTS + 3)

    saves = {}

    def save(key, src, dst, sem):
        saves[key] = pltpu.make_async_copy(src, dst, sem)
        saves[key].start()

    def saved(key):
        if key in saves:
            saves.pop(key).wait()

    for layer in range(LAYERS):
        base = 3 * layer
        arrived(base)
        loads = load_mat(whole, base, mat_c, load_sem)
        for copy in loads:
            copy.start()
        if layer > 0:
            saved("hid")
        hid[...] = stream[...].astype(BF)
        if layer > 0:
            save("hid", hid, hid_out, save_sem.at[0])
        for pair in range(2):
            loads[2 * pair].wait()
            loads[2 * pair + 1].wait()
            hidden = hid[...]
            even = nn(hidden, panel(mat_c[2 * pair, :, :, :, 0:640]))
            odd = nn(hidden, panel(mat_c[2 * pair + 1, :, :, :, 0:640]))
            for tile in range(9):
                if tile < 4:
                    value = even[:, tile * 128 : tile * 128 + 128]
                elif tile == 4:
                    value = jnp.where(low, even[:, 512:640], odd[:, 0:128])
                else:
                    value = odd[:, (tile - 4) * 128 : (tile - 4) * 128 + 128]
                group = pair * 9 + tile
                if group < 6:
                    value = (value + bias[layer, 0:1, group * 128 : group * 128 + 128]).astype(BF)
                    value = value * jnp.asarray(HEAD_DIM**-0.5, BF)
                elif group >= 12:
                    value = value + bias[layer, 1:2, (group - 12) * 128 : (group - 12) * 128 + 128]
                qkv[layer, group] = value.astype(BF)
        clock.until(clock.done + 1)
        save(("qkv", layer), qkv.at[layer], qkv_out.at[layer], save_sem.at[1 + layer])

        if layer > 0:
            saved("ctx")

        def two_heads(pair):
            slot = pair % 2

            @pl.when(pair >= 2)
            def _():
                pltpu.make_async_copy(soft.at[slot], soft_out.at[layer, pl.ds(0, 2)], soft_sem.at[0, slot]).wait()
                if layer == LAYERS - 1:
                    pltpu.make_async_copy(logit.at[slot], logits.at[pl.ds(0, 2)], soft_sem.at[1, slot]).wait()

            values = qkv[layer, 12 + pair]
            keys = qkv[layer, 6 + pair]
            if layer > 0:
                keys = jnp.concatenate([qkv[0, 6 + pair], keys], axis=1)
            for part in range(2):
                rows = pl.ds(part * 256, 256)
                parts = []
                for head in range(2):
                    mine = low if head == 0 else ~low
                    query = jnp.where(mine, qkv[layer, pair, rows, :], jnp.zeros((), BF))
                    if layer > 0:
                        before = jnp.where(mine, qkv[0, pair, rows, :], jnp.zeros((), BF))
                        query = jnp.concatenate([before, query], axis=1)
                    scores = nt(query, keys)
                    if layer == LAYERS - 1:
                        logit[slot, head, rows, :] = scores.astype(BF)
                    scores = scores + penalty[rows, :]
                    powers = jnp.exp(scores - jnp.max(scores, axis=-1, keepdims=True))
                    share = (powers * (1.0 / jnp.sum(powers, axis=-1, keepdims=True))).astype(BF)
                    soft[slot, head, rows, :] = share
                    parts.append(nn(share, values))
                ctx[pair, rows, :] = jnp.where(low, parts[0], parts[1]).astype(BF)
            pltpu.make_async_copy(
                soft.at[slot], soft_out.at[layer, pl.ds(pair * 2, 2)], soft_sem.at[0, slot]
            ).start()
            if layer == LAYERS - 1:
                pltpu.make_async_copy(logit.at[slot], logits.at[pl.ds(pair * 2, 2)], soft_sem.at[1, slot]).start()

        clock.loop(6, two_heads, 3 if layer == 0 else 2)
        for slot in range(2):
            pltpu.make_async_copy(soft.at[slot], soft_out.at[layer, pl.ds(0, 2)], soft_sem.at[0, slot]).wait()
            if layer == LAYERS - 1:
                pltpu.make_async_copy(logit.at[slot], logits.at[pl.ds(0, 2)], soft_sem.at[1, slot]).wait()
        save("ctx", ctx, ctx_out.at[layer], save_sem.at[3])

        arrived(base + 1)
        loads = load_mat(whole, base + 1, mat_u, load_sem)
        for copy in loads:
            copy.start()
        context = jnp.concatenate([ctx[pair] for pair in range(6)], axis=1)
        pieces = []
        for pair in range(2):
            even = nn(context, panel(mat_c[2 * pair, :, :, :, 512:768]))
            odd_far = nn(context, panel(mat_c[2 * pair + 1, :, :, :, 640:768]))
            odd_near = nn(context, panel(mat_c[2 * pair + 1, :, :, :, 0:128]))
            pieces += [even[:, 128:256], turn(jnp.where(low, odd_near, even[:, 0:128])), odd_far]
        first_sum = stream[...] + (jnp.concatenate(pieces, axis=1) + bias[layer, 2:3, :])
        if layer > 0:
            saved("n1")
            saved("nl")
        unit, scale = standardize(first_sum)
        n1[...] = unit
        scale_out[:, 2 * layer : 2 * layer + 1] = scale
        after = unit * gain[layer, 0:1, :] + shift[layer, 0:1, :]
        normed[...] = after
        nl[...] = after.astype(BF)
        save("n1", n1, n1_out.at[layer], save_sem.at[4])
        save("nl", nl, nl_out.at[layer], save_sem.at[5])

        if layer == 0:
            clock.until(clock.done + 1)
        if layer > 0:
            saved("act")
            saved("slope")

        def widen(n):
            wait_for(mat_u.at[n], load_sem.at[n])
            pre = nn(nl[...], panel(mat_u[n])) + up_bias[layer : layer + 1, pl.ds(pl.multiple_of(n * WIDE, WIDE), WIDE)]
            value, slant = gelu_and_slope(pre)
            act[n] = value.astype(BF)
            slope[n] = slant.astype(BF)

        clock.loop(4, widen, 2 if layer == 0 else 3)
        save("act", act, act_out.at[layer], save_sem.at[6])
        save("slope", slope, slope_out.at[layer], save_sem.at[7])
        arrived(base + 2)
        loads = [load_down(whole, base + 2, a, mat_d.at[a], load_sem.at[a]) for a in range(LINES)]
        for copies in loads:
            for copy in copies:
                copy.start()
        if layer > 0:
            saved("n2")
        n2[...] = normed[...] + bias[layer, 3:4, :]

        def narrow_down(a):
            wait_for(mat_d.at[a], load_sem.at[a])
            for b in range(2):
                n2[...] += nt(act[a, :, b * 384 : b * 384 + 384], mat_d[a, b])

        clock.loop(LINES, narrow_down, 1 if layer == 0 else 0)
        unit, scale = standardize(n2[...])
        n2[...] = unit
        scale_out[:, 2 * layer + 1 : 2 * layer + 2] = scale
        after = unit * gain[layer, 1:2, :] + shift[layer, 1:2, :]
        stream[...] = after
        save("n2", n2, n2_out.at[layer], save_sem.at[8])
    result[...] = stream[...].astype(BF)
    for key in list(saves):
        saved(key)
    clock.until(ROUNDS + 3)


def backward_kernel(
    runs, whole, x, hid2, qkv_in, ctx_in, nl_in, act_in, slope_in, n1_in, n2_in, scale_in, soft_in, out_grad, logit_grad,
    gain, *rest
):
    (grad_in, owned, vec, carry, stream, second, go, go_t, nl, nl_t, unit, ctx, gctx, qkv, gqkv, ubuf, dbuf,
     actbuf, slopebuf, soft, dc_in, dc_out, load_sem, misc_sem, soft_sem, grads,
     got1, got2a, got2b, got3, got4, send, recv, free, vec_got, vec_line, vec_send, vec_recv) = rest
    place = Place(runs)
    place.greet()
    clock = Clock(Reduce(place, grads, owned, got1, got2a, got2b, got3, got4, send, recv, free))
    low = low_lanes((1, 128))
    stream[...] = out_grad[...].astype(F32)

    def copies(layer, n, slot):
        return (
            [
                pltpu.make_async_copy(whole.at[3 * layer + 1, :, :, n // 2, n % 2], ubuf.at[slot], load_sem.at[slot, 0]),
                pltpu.make_async_copy(slope_in.at[layer, n], slopebuf.at[slot], load_sem.at[slot, 2]),
            ],
            load_down(whole, 3 * layer + 2, n, dbuf.at[slot], load_sem.at[slot, 3]),
        )

    def act_copy(layer, n, slot):
        return pltpu.make_async_copy(act_in.at[layer, n], actbuf.at[slot], load_sem.at[slot, 1])

    def start_all(layer, n, slot):
        some, more = copies(layer, n, slot)
        for copy in some + more:
            copy.start()

    def wait_all(layer, n, slot):
        for copy in copies(layer, n, slot)[0]:
            copy.wait()
        wait_for(dbuf.at[slot], load_sem.at[slot, 3])

    def norm_back(layer, grad, unit, scale, row):
        vec[row[0] : row[0] + 1, :] = jnp.sum(grad * unit, axis=0, keepdims=True)
        vec[row[1] : row[1] + 1, :] = jnp.sum(grad, axis=0, keepdims=True)
        scaled = grad * gain[layer, row[2] : row[2] + 1, :]
        return (
            scaled
            - jnp.mean(scaled, axis=-1, keepdims=True)
            - unit * jnp.mean(scaled * unit, axis=-1, keepdims=True)
        ) * scale

    ways = [place.at(c=1 - place.c), place.at(y=1 - place.y), place.at(b=1 - place.b)]
    line = vec_line.at[pl.ds(0, LINES - 1)]

    def send_vec(k):
        if k < 3:
            push(vec, vec_got.at[k], vec_send.at[k], vec_recv.at[k], ways[k])
            return
        for o in range(1, LINES):
            push(vec, vec_line.at[place.a], vec_send.at[3], vec_recv.at[3], place.at(a=(place.a + o) % LINES))

    def add_vec(k):
        if k < 3:
            wait_for(vec, vec_send.at[k])
            wait_for(vec_got.at[k], vec_recv.at[k])
            vec[...] += vec_got[k]
            return
        wait_for(line, vec_send.at[3])
        wait_for(line, vec_recv.at[3])
        vec_line[place.a] = vec[...]
        vec[...] = (vec_line[0] + vec_line[1]) + (vec_line[2] + vec_line[3])

    for layer in reversed(range(LAYERS)):
        base = 12 * layer
        early = [
            pltpu.make_async_copy(n2_in.at[layer], unit, misc_sem.at[0]),
            pltpu.make_async_copy(nl_in.at[layer], nl, misc_sem.at[1]),
            pltpu.make_async_copy(ctx_in.at[layer], ctx, misc_sem.at[2]),
            pltpu.make_async_copy(qkv_in.at[layer], qkv, misc_sem.at[3]),
        ]
        act_copy(layer, 0, 0).start()
        for copy in early:
            copy.start()
        start_all(layer, 0, 0)
        for copy in early[:2]:
            copy.wait()
        second[...] = norm_back(
            layer, stream[...], unit[...], scale_in[:, 2 * layer + 1 : 2 * layer + 2], (base + 9, base + 11, 1)
        )
        go[...] = second[...].astype(BF)
        go_t[...] = go[...].T
        nl_t[...] = nl[...].T
        late = [
            pltpu.make_async_copy(n1_in.at[layer], unit, misc_sem.at[0]),
            pltpu.make_async_copy(hid2 if layer == 1 else x, nl, misc_sem.at[1]),
        ]
        for copy in late:
            copy.start()
        vec[base + 3 : base + 4, :] = jnp.sum(go[...].astype(F32), axis=0, keepdims=True)
        stream[...] = second[...]
        if layer == 1:
            place.meet()
        clock.until(0 if layer == 1 else PARTS + 1)

        def down_grad(n):
            slot = n % 2
            act_copy(layer, n, slot).wait()

            @pl.when(n < 3)
            def _():
                act_copy(layer, n + 1, 1 - slot).start()

            for b in range(2):
                down = nn(go_t[...], actbuf[slot, :, b * 384 : b * 384 + 384]).astype(BF)
                for m in range(4):
                    for h in range(2):
                        grads[2, n, b, m // 2, m % 2, :, h * 384 : h * 384 + 384] = down[
                            192 * m + BLOCK * h : 192 * m + BLOCK * h + BLOCK, :
                        ]

        clock.loop(4, down_grad, 0 if layer == 1 else 1)
        clock.until(1 if layer == 1 else 2 * PARTS + 1)

        def chunk(n):
            slot = n % 2
            wait_all(layer, n, slot)

            @pl.when(n < 3)
            def _():
                start_all(layer, n + 1, 1 - slot)

            outer = go[...]
            wide = jnp.concatenate([nn(outer, dbuf[slot, 0]), nn(outer, dbuf[slot, 1])], axis=1)
            pre = (wide * slopebuf[slot].astype(F32)).astype(BF)
            vec[pl.ds(base + 4 + n, 1), :] = jnp.sum(pre.astype(F32), axis=0, keepdims=True)
            stream[...] += nt(pre, panel(ubuf[slot]))
            up = nn(nl_t[...], pre).astype(BF)
            grads[1, :, :, n // 2, n % 2] = up.reshape(LINES, 2, BLOCK, WIDE)

        clock.loop(4, chunk, 2 if layer == 1 else 4)

        def side_copy(n):
            return pltpu.make_async_copy(whole.at[3 * layer, :, :, n // 2, n % 2], ubuf.at[n % 2], load_sem.at[n % 2, 0])

        side_copy(0).start()
        side_copy(1).start()
        for copy in late + early[2:]:
            copy.wait()
        second[...] = norm_back(layer, stream[...], unit[...], scale_in[:, 2 * layer : 2 * layer + 1], (base + 8, base + 10, 0))
        go[...] = second[...].astype(BF)
        vec[base + 2 : base + 3, :] = jnp.sum(go[...].astype(F32), axis=0, keepdims=True)

        def tile_of(index):
            return go[:, index * 128 : index * 128 + 128]

        zero = jnp.zeros((), BF)
        outs = []
        for pair in range(2):
            mixed = turn(tile_of(3 * pair + 1).astype(F32)).astype(BF)
            outs.append((jnp.where(low, zero, mixed), tile_of(3 * pair)))
            outs.append((jnp.where(low, mixed, zero), tile_of(3 * pair + 2)))
        stream[...] = jnp.zeros_like(stream)
        for n in range(4):
            near = slice(512, 640) if n % 2 == 0 else slice(0, 128)
            side_copy(n).wait()
            stream[...] += nt(outs[n][0], panel(ubuf[n % 2, :, :, :, near])) + nt(
                outs[n][1], panel(ubuf[n % 2, :, :, :, 640:768])
            )
            side_copy((n + 2) % 4).start()
        for pair in range(6):
            gctx[pair] = stream[:, pair * 128 : pair * 128 + 128].astype(BF)

        if layer == 1:
            clock.until(PARTS + 1)
        above = logit_grad if layer == LAYERS - 1 else carry

        def fetch(pair, slot):
            return [
                pltpu.make_async_copy(soft_in.at[layer, pl.ds(pair * 2, 2)], soft.at[slot], soft_sem.at[0, slot]),
                pltpu.make_async_copy(above.at[pl.ds(pair * 2, 2)], dc_in.at[slot], soft_sem.at[1, slot]),
            ]

        for copy in fetch(0, 0):
            copy.start()

        def two_heads(pair):
            slot = pair % 2
            for copy in fetch(pair, slot):
                copy.wait()

            @pl.when(pair < 5)
            def _():
                for copy in fetch(pair + 1, 1 - slot):
                    copy.start()

            if layer > 0:

                @pl.when(pair >= 2)
                def _():
                    pltpu.make_async_copy(dc_out.at[slot], carry.at[pl.ds(0, 2)], soft_sem.at[2, slot]).wait()

            queries, keys, values, grad = qkv[pair], qkv[6 + pair], qkv[12 + pair], gctx[pair]
            both = grad.astype(F32) * ctx[pair].astype(F32)
            grad_q, grad_k, grad_v = 0.0, 0.0, 0.0
            for head in range(2):
                mine = low if head == 0 else ~low
                own = jnp.where(mine, grad, zero)
                dot = jnp.sum(jnp.where(mine, both, 0.0), axis=-1, keepdims=True)
                share = soft[slot, head]
                inner = nt(own, values)
                scores = (share.astype(F32) * (inner - dot) + dc_in[slot, head].astype(F32)).astype(BF)
                dc_out[slot, head] = scores
                grad_v = grad_v + tn(share, own)
                grad_q = grad_q + nn(scores, jnp.where(mine, keys, zero))
                grad_k = grad_k + tn(scores, jnp.where(mine, queries, zero))
            gqkv[pair] = (grad_q * HEAD_DIM**-0.5).astype(BF)
            gqkv[6 + pair] = grad_k.astype(BF)
            gqkv[12 + pair] = grad_v.astype(BF)
            if layer > 0:
                pltpu.make_async_copy(dc_out.at[slot], carry.at[pl.ds(pair * 2, 2)], soft_sem.at[2, slot]).start()

        clock.loop(6, two_heads, 2 if layer == 1 else 3)
        if layer > 0:
            for slot in range(2):
                pltpu.make_async_copy(dc_out.at[slot], carry.at[pl.ds(0, 2)], soft_sem.at[2, slot]).wait()
        for group in range(6):
            lanes = slice(group * 128, group * 128 + 128)
            vec[base : base + 1, lanes] = jnp.sum(gqkv[group].astype(F32), axis=0, keepdims=True)
            vec[base + 1 : base + 2, lanes] = jnp.sum(gqkv[12 + group].astype(F32), axis=0, keepdims=True)

        if layer == 0:
            send_vec(0)

        nl_t[...] = nl[...].T
        go_t[...] = jnp.concatenate([ctx[pair] for pair in range(6)], axis=1).T
        clock.until(2 * PARTS if layer == 1 else 3 * PARTS + 1)
        stream[...] = second[...]
        for n in range(4):
            pair = n // 2
            if n % 2 == 0:
                tiles = [gqkv[9 * pair + k] for k in range(4)] + [jnp.where(low, gqkv[9 * pair + 4], zero)]
            else:
                tiles = [jnp.where(low, zero, gqkv[9 * pair + 4])] + [gqkv[9 * pair + k] for k in range(5, 9)]
            side = jnp.concatenate(tiles, axis=1)
            side_copy(n).wait()
            stream[...] += nt(side, panel(ubuf[n % 2, :, :, :, 0:640]))
            if n < 2:
                side_copy(n + 2).start()
            first = nn(nl_t[...], side)
            near = nn(go_t[...], outs[n][0])
            far = nn(go_t[...], outs[n][1])
            shape = (LINES, 2, BLOCK, 128)
            mixed = 4 if n % 2 == 0 else 0
            for tile in range(5):
                value = first[:, tile * 128 : tile * 128 + 128]
                if tile == mixed:
                    value = value + near
                grads[0, :, :, n // 2, n % 2, :, tile * 128 : tile * 128 + 128] = value.astype(BF).reshape(shape)
            grads[0, :, :, n // 2, n % 2, :, 640:768] = far.astype(BF).reshape(shape)
            if layer == 0:
                if n % 2 == 1:
                    add_vec(n // 2)
                    send_vec(n // 2 + 1)
    grad_in[...] = stream[...].astype(BF)
    clock.until(ROUNDS - 2)
    add_vec(2)
    send_vec(3)
    clock.until(ROUNDS)
    add_vec(3)
    clock.until(ROUNDS + GAP + 4)


def forward(runs, mats, x, segments, bias, up_bias, gain, shift):
    length, width = x.shape
    heads = width // HEAD_DIM
    sds = jax.ShapeDtypeStruct
    vmem, hbm = pl.BlockSpec(memory_space=pltpu.VMEM), pl.BlockSpec(memory_space=pltpu.HBM)
    outs = [
        (sds((length, width), BF), vmem),
        (sds((heads, length, length), BF), hbm),
        (sds((LAYERS, heads, length, length), BF), hbm),
        (sds((LAYERS, 18, length, 128), BF), hbm),
        (sds((LAYERS, 6, length, 128), BF), hbm),
        (sds((length, width), BF), hbm),
        (sds((LAYERS, length, width), BF), hbm),
        (sds((LAYERS, 4, length, width), BF), hbm),
        (sds((LAYERS, 4, length, width), BF), hbm),
        (sds((LAYERS, length, width), F32), hbm),
        (sds((LAYERS, length, width), F32), hbm),
        (sds((length, 2 * LAYERS), F32), vmem),
    ]
    outs.append((sds((6, LINES, 2, 2, 2, BLOCK, WIDE), BF), hbm))
    dma = pltpu.SemaphoreType.DMA
    scratch = [
        pltpu.VMEM((length, width), F32),
        pltpu.VMEM((LAYERS, 18, length, 128), BF),
        pltpu.VMEM((6, length, 128), BF),
        pltpu.VMEM((length, width), F32),
        pltpu.VMEM((length, width), F32),
        pltpu.VMEM((length, width), F32),
        pltpu.VMEM((length, width), BF),
        pltpu.VMEM((length, width), BF),
        pltpu.VMEM((4, length, width), BF),
        pltpu.VMEM((4, length, width), BF),
        pltpu.VMEM((length, length), F32),
        pltpu.VMEM((2, 2, length, length), BF),
        pltpu.VMEM((2, 2, length, length), BF),
        pltpu.VMEM((4, LINES, 2, BLOCK, WIDE), BF),
        pltpu.VMEM((4, LINES, 2, BLOCK, WIDE), BF),
        pltpu.VMEM((LINES, 2, WIDE, 384), BF),
        dma((4,)),
        dma((2, 2)),
        dma((9,)),
        dma(()),
        dma((ROUNDS, 2, 4)),
        dma((ROUNDS, 2, 7)),
        pltpu.VMEM((6, BLOCK, WIDE), BF),
        pltpu.VMEM((BLOCK, 640), F32),
        pltpu.VMEM((BLOCK, 256), F32),
    ]
    return pl.pallas_call(
        functools.partial(forward_kernel, runs),
        out_shape=[o[0] for o in outs],
        in_specs=[vmem] * 10,
        out_specs=[o[1] for o in outs],
        scratch_shapes=scratch,
        compiler_params=pltpu.CompilerParams(vmem_limit_bytes=60 << 20, collective_id=0, has_side_effects=True),
        name="ahead",
    )(*mats, x, segments, bias, up_bias, gain, shift)


def backward(runs, whole, x, kept, out_grad, logit_grad, gain):
    soft, qkv, ctx, hid2, nl, act, slope, n1, n2, scale = kept
    length, width = x.shape
    heads = width // HEAD_DIM
    sds = jax.ShapeDtypeStruct
    vmem, hbm = pl.BlockSpec(memory_space=pltpu.VMEM), pl.BlockSpec(memory_space=pltpu.HBM)
    blocks = (LINES, 2, 2, 2, BLOCK, WIDE)
    outs = [
        (sds((length, width), BF), vmem),
        (sds((6, BLOCK, WIDE), F32), vmem),
        (sds((12 * LAYERS, width), F32), vmem),
        (sds((heads, length, length), BF), hbm),
    ]
    dma = pltpu.SemaphoreType.DMA
    scratch = [
        pltpu.VMEM((length, width), F32),
        pltpu.VMEM((length, width), F32),
        pltpu.VMEM((length, width), BF),
        pltpu.VMEM((width, length), BF),
        pltpu.VMEM((length, width), BF),
        pltpu.VMEM((width, length), BF),
        pltpu.VMEM((length, width), F32),
        pltpu.VMEM((6, length, 128), BF),
        pltpu.VMEM((6, length, 128), BF),
        pltpu.VMEM((18, length, 128), BF),
        pltpu.VMEM((18, length, 128), BF),
        pltpu.VMEM((2, LINES, 2, BLOCK, WIDE), BF),
        pltpu.VMEM((2, 2, WIDE, 384), BF),
        pltpu.VMEM((2, length, width), BF),
        pltpu.VMEM((2, length, width), BF),
        pltpu.VMEM((2, 2, length, length), BF),
        pltpu.VMEM((2, 2, length, length), BF),
        pltpu.VMEM((2, 2, length, length), BF),
        dma((2, 4)),
        dma((4,)),
        dma((3, 2)),
        pltpu.VMEM((3,) + blocks, BF),
        pltpu.VMEM((SETS, 2, 2, LINES, 2, PIECE, WIDE), BF),
        pltpu.VMEM((SETS, LINES, 2, PIECE, WIDE), BF),
        pltpu.VMEM((SETS, 2, LINES, PIECE, WIDE), BF),
        pltpu.VMEM((SETS, 2, LINES, PIECE, WIDE), BF),
        pltpu.VMEM((SETS, 2, LINES - 1, PIECE, WIDE), BF),
        dma((SETS, 2, 4)),
        dma((SETS, 2, 4)),
        pltpu.SemaphoreType.REGULAR((SETS,)),
        pltpu.VMEM((3, 12 * LAYERS, width), F32),
        pltpu.VMEM((LINES, 12 * LAYERS, width), F32),
        dma((4,)),
        dma((4,)),
    ]
    return pl.pallas_call(
        functools.partial(backward_kernel, runs),
        out_shape=[o[0] for o in outs],
        in_specs=[hbm] * 10 + [vmem, hbm, vmem, hbm, vmem],
        out_specs=[o[1] for o in outs],
        scratch_shapes=scratch,
        compiler_params=pltpu.CompilerParams(vmem_limit_bytes=62 << 20, collective_id=1, has_side_effects=True),
        name="back",
    )(whole, x, hid2, qkv, ctx, nl, act, slope, n1, n2, scale, soft, out_grad, logit_grad, gain)


def finish_kernel(owned, vec, result_in, grad_in, logits_in, result, logits, grad, g_qkv, g_out, g_up, g_down,
                  g_bias, g_up_bias, g_gain, g_shift, stage, sem):
    heads = logits.shape[0]
    count = stage.shape[0]
    step = heads // count
    parts = [pl.ds(k * step, step) for k in range(count)]
    for k, at in enumerate(parts):
        pltpu.make_async_copy(logits_in.at[at], stage.at[k], sem.at[0, k]).start()
    result[...] = result_in[...]
    grad[...] = grad_in[...]
    odd = lax.broadcasted_iota(jnp.int32, (1, 128), 1) * 0 + lax.axis_index("narrow") % 2 == 1
    low = low_lanes((1, 128))
    for layer in range(LAYERS):
        block = owned[3 * layer]
        moved = pltpu.roll(block, WIDE - HEAD_DIM, 1)
        for k in range(5):
            lanes = slice(k * 128, min(k * 128 + 128, 576))
            tile = slice(k * 128, k * 128 + 128)
            g_qkv[layer, :, lanes] = jnp.where(odd, moved[:, tile], block[:, tile])[:, : lanes.stop - lanes.start]
        last = block[:, 640:768]
        g_out[layer, :, 0:128] = jnp.where(odd, jnp.where(low, block[:, 0:128], turn(last)), last)
        g_out[layer, :, 128:192] = jnp.where(odd, turn(last), turn(block[:, 512:640]))[:, 0:64]
        g_up[layer] = owned[3 * layer + 1]
        down = owned[3 * layer + 2]
        g_down[layer, 0:BLOCK, :] = down[:, 0:384]
        g_down[layer, BLOCK : 2 * BLOCK, :] = down[:, 384:768]
        base = 12 * layer
        g_bias[layer] = vec[base : base + 4, :]
        for n in range(4):
            g_up_bias[layer : layer + 1, n * WIDE : n * WIDE + WIDE] = vec[base + 4 + n : base + 5 + n, :]
        g_gain[layer] = vec[base + 8 : base + 10, :]
        g_shift[layer] = vec[base + 10 : base + 12, :]
    for k, at in enumerate(parts):
        pltpu.make_async_copy(logits_in.at[at], stage.at[k], sem.at[0, k]).wait()
        pltpu.make_async_copy(stage.at[k], logits.at[at], sem.at[1, k]).start()
    for k, at in enumerate(parts):
        pltpu.make_async_copy(stage.at[k], logits.at[at], sem.at[1, k]).wait()


def finish(owned, vec, result, grad, logits):
    sds = jax.ShapeDtypeStruct
    vmem, hbm = pl.BlockSpec(memory_space=pltpu.VMEM), pl.BlockSpec(memory_space=pltpu.HBM)
    heads, length, _ = logits.shape
    outs = [
        (sds(result.shape, BF), vmem),
        (sds(logits.shape, BF), hbm),
        (sds(grad.shape, BF), vmem),
        (sds((LAYERS, BLOCK, 576), F32), vmem),
        (sds((LAYERS, BLOCK, 192), F32), vmem),
        (sds((LAYERS, BLOCK, WIDE), F32), vmem),
        (sds((LAYERS, 2 * BLOCK, 384), F32), vmem),
        (sds((LAYERS, 4, WIDE), F32), vmem),
        (sds((LAYERS, 4 * WIDE), F32), vmem),
        (sds((LAYERS, 2, WIDE), F32), vmem),
        (sds((LAYERS, 2, WIDE), F32), vmem),
    ]
    return pl.pallas_call(
        finish_kernel,
        out_shape=[o[0] for o in outs],
        in_specs=[vmem] * 4 + [hbm],
        out_specs=[o[1] for o in outs],
        scratch_shapes=[pltpu.VMEM((6, heads // 6, length, length), BF), pltpu.SemaphoreType.DMA((2, 6))],
        compiler_params=pltpu.CompilerParams(vmem_limit_bytes=48 << 20),
        name="finish",
    )(owned, vec, result, grad, logits)


def body(runs, inputs, segments, out_grad, logit_grad, w_qkv, w_out, w_up, w_down, biases, up_bias, gains, shifts):
    mats = [w_qkv, w_out, w_up, w_down]
    groups = [[g * runs + r for r in range(runs)] for g in range(2 * LINES)]
    if runs > 1:
        mats = [lax.all_gather(w.astype(BF), "dp", axis_index_groups=groups, axis=1, tiled=True) for w in mats]
    result, logits, *kept, whole = forward(runs, mats[:3] + [jnp.swapaxes(mats[3], 1, 2)], inputs[0], segments, biases, up_bias, gains, shifts)
    grad_in, owned, vec, _ = backward(runs, whole, inputs[0], kept, out_grad[0], logit_grad[0], gains)
    result, logits, grad_in, *grads = finish(owned, vec, result, grad_in, logits)
    grads[3] = jnp.swapaxes(grads[3], 1, 2)
    if runs > 1:
        grads = [
            lax.psum_scatter(g, "dp", axis_index_groups=groups, scatter_dimension=1, tiled=True) for g in grads[:4]
        ] + list(lax.psum(tuple(grads[4:]), "dp", axis_index_groups=groups))
    return (result[None], logits[None], grad_in[None], *grads)


def solution(mesh):
    rows = P(("dp", "narrow"), None, None)
    heads = P(("dp", "narrow"), None, None, None)
    blocks = P(None, "dp", "narrow")
    runs = mesh.shape["dp"] // (2 * LINES)
    return jax.shard_map(
        functools.partial(body, runs),
        mesh=mesh,
        in_specs=(rows, P(("dp", "narrow"), None), rows, heads) + (blocks,) * 4 + (P(),) * 4,
        out_specs=(rows, heads, rows) + (blocks,) * 4 + (P(),) * 4,
        check_vma=False,
    )
```
